512 devices in a mesh: ia: 64 (over x, z_lo, core), ja: 8 (over y, z_hi).
Axes of the slice: x: 4, y: 4, z: 16 (z_hi: 2, z_lo: 8; z = z_hi * 8 + z_lo), core: 2. Of those that a mesh axis runs over, the one named last changes fastest.
Arguments:
- state: bfloat16 [64, 2048, 384], P('ja', 'ia')
- cotangent: bfloat16 [64, 2048, 384], P('ja', 'ia'), may hold values from -6 to 6
- ocean: int32 [64, 2048], P('ja', 'ia'), may hold values from 0 to 1, as said below
- fold_partner: int32 [64], P('ia'), may hold values from 0 to 63, as said below
- kernel: float32 [49, 384], replicated, may hold values from -0.875 to 0.875
- ln_gain: float32 [384], replicated, may hold values from 0.25 to 1.75
- ln_shift: float32 [384], replicated, may hold values from -3 to 3
- w_up: bfloat16 [384, 768], replicated, may hold values from -0.3125 to 0.3125
- b_up: float32 [768], replicated, may hold values from -3 to 3
- w_down: bfloat16 [384, 768], replicated, may hold values from -0.21875 to 0.21875
- b_down: float32 [384], replicated, may hold values from -3 to 3
- layer_scale: float32 [384], replicated, may hold values from 0.5 to 2
Outputs:
- grad_state: bfloat16 [64, 2048, 384], P('ja', 'ia')
- grad_w_up: float32 [384, 768], P('ja', 'ia')
- grad_w_down: float32 [384, 768], P('ja', 'ia')
- grad_kernel: float32 [49, 384], replicated
- grad_channels: float32 [4, 384], replicated
- grad_b_up: float32 [768], replicated
The draws below stay inside these ranges and needn't reach their ends.
Inputs may be any that keep to these rules, and one draw needn't show every extreme that they name: Within aligned tiles of 8 rows by 32 columns each cell is ocean with a probability drawn per tile from 0, 1/4, 1/2, 3/4 and 1. fold_partner[s] = (K - s) mod 64 for one K.
All inputs are finite; a program needn't handle non-finite values.
Results may differ from the reference program's by a relative error of at most 0.0063.
Values may be sent and summed in bfloat16 or wider, within the bound.
A program may use at most 64 MiB of HBM per device.

```python
import math
import jax
import jax.numpy as jnp
from jax import lax

C = 384
HID = 768
KWIDTH = 7
CI = 32
NJ = 64
NI = 2048
LANES = 64


def draw_state(key, part):
    key = jax.random.fold_in(key, 11)
    first, second = jax.random.split(key, 2)
    chan = jnp.exp(jax.random.uniform(second, (C,), jnp.float32, math.log(0.3), math.log(3.0)))
    values = jax.random.normal(first, (NJ, NI, C), jnp.float32) * chan
    return values.astype(jnp.bfloat16)


def draw_ocean(key, part):
    key = jax.random.fold_in(key, 23)
    first, second = jax.random.split(key)
    level = jax.random.randint(first, (NJ // 8, NI // 32), 0, 5)
    level = jnp.repeat(jnp.repeat(level, 8, axis=0), 32, axis=1)
    pick = jax.random.randint(second, (NJ, NI), 0, 4)
    return (pick < level).astype(jnp.int32)


def draw_fold_partner(key, part):
    key = jax.random.fold_in(key, 37)
    pivot = jax.random.randint(key, (), 0, LANES)
    return ((pivot - jnp.arange(LANES, dtype=jnp.int32)) % LANES).astype(jnp.int32)


def strengthened(array, stream_key, source, target, shards_of, factor):
    def block_of(position):
        return (jnp.arange(array.shape[position]) // (array.shape[position] // shards_of)).reshape((-1,) + (1,) * (array.ndim - 1 - position))

    first = jax.random.permutation(stream_key, shards_of)[block_of(target)]
    other_side = (block_of(target) + shards_of // 2) % shards_of
    return jnp.where((block_of(source) == first) | (block_of(source) == other_side), factor * array, array)


def block_levels(stream_key, dims, shards, smallest, high):
    def one(axis_at, shards_of):
        heights = jax.random.uniform(jax.random.fold_in(jax.random.fold_in(stream_key, 6), axis_at), (shards_of,), jnp.float32, smallest / len(shards), high / len(shards))
        return jnp.repeat(jnp.exp(heights), dims[axis_at] // shards_of).reshape((-1,) + (1,) * (len(dims) - axis_at - 1))

    level = one(*shards[0])
    for cut in shards[1:]:
        level = level * one(*cut)
    return level


def noise(key, extent, width, reach, pieces=(), kind=jnp.bfloat16):
    values = jax.random.normal(key, extent, jnp.float32) * width
    if len(pieces) > 0:
        values = block_levels(key, extent, pieces, -0.22, 0.18) * values
    return jnp.clip(values, min=-reach, max=reach).astype(kind)


def noise_with(rng, dims, scale, most, shards, heavy, kind=jnp.bfloat16):
    result = scale * jax.random.normal(rng, dims, jnp.float32)
    if shards:
        result = result * block_levels(rng, dims, shards, -0.22, 0.18)
    return jnp.clip(strengthened(result, jax.random.fold_in(rng, 3), *heavy), -most, most).astype(kind)


def setup_inputs(seed: int = 0) -> dict:
    arg_keys = jax.random.split(jax.random.key(seed), 13)
    return {
        "state": draw_state(jax.random.fold_in(arg_keys[12], 71), 0),
        "cotangent": noise_with(arg_keys[1], (NJ, NI, C), 1.0, 6.0, ((0, 8), (1, 64)), (0, 2, 8, 2.0)),
        "ocean": draw_ocean(jax.random.fold_in(arg_keys[12], 71), 0),
        "fold_partner": draw_fold_partner(jax.random.fold_in(arg_keys[12], 71), 0),
        "kernel": noise(arg_keys[4], (KWIDTH * KWIDTH, C), (KWIDTH * KWIDTH) ** -0.5, 0.875, (), jnp.float32),
        "ln_gain": jnp.clip(1.0 + 0.15 * jax.random.normal(arg_keys[5], (C,), jnp.float32), 0.25, 1.75),
        "ln_shift": noise(arg_keys[6], (C,), 0.5, 3.0, (), jnp.float32),
        "w_up": noise(arg_keys[7], (C, HID), C ** -0.5, 0.3125),
        "b_up": noise(arg_keys[8], (HID,), 0.5, 3.0, (), jnp.float32),
        "w_down": noise(arg_keys[9], (C, HID), HID ** -0.5, 0.21875),
        "b_down": noise(arg_keys[10], (C,), 0.5, 3.0, (), jnp.float32),
        "layer_scale": jnp.clip(jnp.exp(jax.random.uniform(arg_keys[11], (C,), jnp.float32, math.log(0.5), math.log(2.0))), 0.5, 2.0),
    }


def gelu_parts(pre):
    coeff = 0.7978845608028654
    inner = coeff * (pre + 0.044715 * pre * pre * pre)
    tanh_value = jnp.tanh(inner)
    value = 0.5 * pre * (1.0 + tanh_value)
    slope = 0.5 * (1.0 + tanh_value) + 0.5 * pre * (1.0 - tanh_value * tanh_value) * coeff * (1.0 + 3.0 * 0.044715 * pre * pre)
    return (value, slope)

def depthwise(padded, taps, rows, cols):
    total = jnp.zeros((rows, cols, padded.shape[2]), jnp.float32)
    for first in range(KWIDTH):
        for second in range(KWIDTH):
            total = total + padded[first:first + rows, second:second + cols].astype(jnp.float32) * taps[first * KWIDTH + second]
    return total

def block_grads(padded, cotangent, ocean, kernel, ln_gain, ln_shift, w_up, b_up, w_down, b_down, layer_scale, rows, cols):
    chans = padded.shape[2]
    cells = rows * cols
    conv = depthwise(padded, kernel, rows, cols).reshape(cells, chans)
    centred = conv - lax.optimization_barrier(jnp.mean(conv, axis=1, keepdims=True))
    rstd = lax.rsqrt(lax.optimization_barrier(jnp.mean(centred * centred, axis=1, keepdims=True)) + 1e-06)
    unit = centred * rstd
    normed = (unit * ln_gain + ln_shift).astype(jnp.bfloat16)
    pre = jnp.dot(normed, w_up, preferred_element_type=jnp.float32) + b_up
    act, slope = gelu_parts(pre)
    hidden = act.astype(jnp.bfloat16)
    branch = lax.dot_general(hidden, w_down, (((1,), (1,)), ((), ())), preferred_element_type=jnp.float32) + b_down
    masked = cotangent.reshape(cells, chans).astype(jnp.float32) * ocean.reshape(cells, 1).astype(jnp.float32)
    d_branch = masked * layer_scale
    d_branch_b = d_branch.astype(jnp.bfloat16)
    g_scale = lax.optimization_barrier(jnp.sum(masked * branch, axis=0))
    g_bdown = lax.optimization_barrier(jnp.sum(d_branch, axis=0))
    g_wdown = lax.dot_general(d_branch_b, hidden, (((0,), (0,)), ((), ())), preferred_element_type=jnp.float32)
    d_hidden = jnp.dot(d_branch_b, w_down, preferred_element_type=jnp.float32)
    d_pre = d_hidden * slope
    d_pre_b = d_pre.astype(jnp.bfloat16)
    g_bup = lax.optimization_barrier(jnp.sum(d_pre, axis=0))
    g_wup = lax.dot_general(normed, d_pre_b, (((0,), (0,)), ((), ())), preferred_element_type=jnp.float32)
    d_normed = lax.dot_general(d_pre_b, w_up, (((1,), (1,)), ((), ())), preferred_element_type=jnp.float32)
    g_gain = lax.optimization_barrier(jnp.sum(d_normed * unit, axis=0))
    g_shift = lax.optimization_barrier(jnp.sum(d_normed, axis=0))
    scaled = d_normed * ln_gain
    d_conv = rstd * (scaled - lax.optimization_barrier(jnp.mean(scaled, axis=1, keepdims=True)) - unit * lax.optimization_barrier(jnp.mean(scaled * unit, axis=1, keepdims=True)))
    d_conv_b = d_conv.astype(jnp.bfloat16).reshape(rows, cols, chans)
    d_conv_f = d_conv_b.astype(jnp.float32)
    g_kernel = jnp.stack([lax.optimization_barrier(jnp.sum(padded[first:first + rows, second:second + cols].astype(jnp.float32) * d_conv_f, axis=(0, 1))) for first in range(KWIDTH) for second in range(KWIDTH)])
    g_chan = jnp.stack([g_gain, g_shift, g_bdown, g_scale])
    return (d_conv_b, (g_wup, g_wdown, g_kernel, g_chan, g_bup))

def reference(state, cotangent, ocean, fold_partner, kernel, ln_gain, ln_shift, w_up, b_up, w_down, b_down, layer_scale):
    pad = KWIDTH // 2
    pivot = fold_partner[0] * CI + CI - 1
    wide_cols = ((pivot - (jnp.arange(NI + 2 * pad, dtype=jnp.int32) - pad)) % NI).astype(jnp.int32)
    grid_cols = ((pivot - jnp.arange(NI, dtype=jnp.int32)) % NI).astype(jnp.int32)
    wide = jnp.concatenate([state[:, NI - pad:], state, state[:, :pad]], axis=1)
    ghost = jnp.take(state[NJ - 1 - pad:NJ - 1][::-1], wide_cols, axis=1)
    padded = jnp.concatenate([jnp.zeros((pad, NI + 2 * pad, C), jnp.bfloat16), wide, ghost], axis=0)
    rows = 8
    count = NJ // rows

    def forward_step(carry, index):
        start = index * rows
        window = lax.dynamic_slice_in_dim(padded, start, rows + 2 * pad, 0)
        grads = lax.dynamic_slice_in_dim(cotangent, start, rows, 0)
        land = lax.dynamic_slice_in_dim(ocean, start, rows, 0)
        d_conv, terms = block_grads(window, grads, land, kernel, ln_gain, ln_shift, w_up, b_up, w_down, b_down, layer_scale, rows, NI)
        return (tuple((total + term for total, term in zip(carry, terms))), d_conv)
    init = (jnp.zeros((C, HID), jnp.float32), jnp.zeros((C, HID), jnp.float32), jnp.zeros((KWIDTH * KWIDTH, C), jnp.float32), jnp.zeros((4, C), jnp.float32), jnp.zeros((HID,), jnp.float32))
    sums, d_blocks = lax.scan(forward_step, init, jnp.arange(count, dtype=jnp.int32))
    d_conv = d_blocks.reshape(NJ, NI, C)
    d_wide = jnp.concatenate([d_conv[:, NI - pad:], d_conv, d_conv[:, :pad]], axis=1)
    d_padded = jnp.concatenate([jnp.zeros((pad, NI + 2 * pad, C), jnp.bfloat16), d_wide, jnp.zeros((2 * pad, NI + 2 * pad, C), jnp.bfloat16)], axis=0)
    flipped = kernel[::-1]
    beyond = depthwise(d_padded[NJ:], flipped, pad, NI)
    fold = jnp.take(beyond[::-1], grid_cols, axis=1)
    extra = jnp.concatenate([jnp.zeros((rows - 1 - pad, NI, C), jnp.float32), fold, jnp.zeros((1, NI, C), jnp.float32)], axis=0)

    def back_step(carry, index):
        start = index * rows
        window = lax.dynamic_slice_in_dim(d_padded, start, rows + 2 * pad, 0)
        grads = lax.dynamic_slice_in_dim(cotangent, start, rows, 0).astype(jnp.float32)
        total = grads + depthwise(window, flipped, rows, NI)
        total = total + jnp.where(index == count - 1, extra, jnp.zeros_like(extra))
        return (carry, total.astype(jnp.bfloat16))
    _, x_blocks = lax.scan(back_step, jnp.zeros((), jnp.float32), jnp.arange(count, dtype=jnp.int32))
    grad_state = x_blocks.reshape(NJ, NI, C)
    factor = 1.0 / math.sqrt(NJ * NI)
    g_wup, g_wdown, g_kernel, g_chan, g_bup = sums
    return (grad_state, g_wup * factor, g_wdown * factor, g_kernel * factor, g_chan * factor, g_bup * factor)
```

```python
import functools
import math

import jax
import jax.numpy as jnp
from jax import lax
from jax.experimental import pallas as pl
from jax.experimental.pallas import tpu as pltpu
from jax.sharding import PartitionSpec as P

KW = 7
PAD = 3
ROWS = 8
COLS = 32
CH = 384
HID = 768
CELLS = ROWS * COLS
WIDE = 48
F32 = jnp.float32
BF16 = jnp.bfloat16
LANES = 64
BANDS = 8
COEFF = 0.7978845608028654
CUBIC = 0.044715
FACTOR = 1.0 / math.sqrt(ROWS * BANDS * COLS * LANES)


def place(x, y, z, c):
    return {"ia": x * 16 + lax.rem(z, 8) * 2 + c, "ja": y * 2 + z // 8}


def dot(a, b, dims=(1, 0)):
    return lax.dot_general(
        a, b, (((dims[0],), (dims[1],)), ((), ())), preferred_element_type=F32
    )


def sub8(v):
    return v[0:8] + v[8:16] + v[16:24] + v[24:32]


def onehot(rows, cols, target):
    want = target(lax.broadcasted_iota(jnp.int32, (1, cols), 1))
    here = lax.broadcasted_iota(jnp.int32, (rows, cols), 0)
    return jnp.where(here == want, 1.0, 0.0).astype(BF16)


def split3(v):
    hi = v.astype(BF16)
    rest = v - hi.astype(F32)
    mid = rest.astype(BF16)
    low = (rest - mid.astype(F32)).astype(BF16)
    zeros = jnp.zeros((13, v.shape[1]), F32)
    return jnp.concatenate(
        [hi.astype(F32), mid.astype(F32), low.astype(F32), zeros], axis=0
    ).astype(BF16)


def conv_into(wide, taps, flip, write):
    def tile(ct, _):
        lanes = pl.ds(pl.multiple_of(ct * 128, 128), 128)
        total = [jnp.zeros((COLS, 128), F32) for _ in range(ROWS)]
        for b in range(KW):
            weight = []
            for a in range(KW):
                tap = a * KW + b
                tap = KW * KW - 1 - tap if flip else tap
                weight.append(taps[tap : tap + 1, lanes])
            for r in range(ROWS + 2 * PAD):
                value = wide[ct, r, 5 + b : 5 + b + COLS, :]
                for a in range(KW):
                    j = r - a
                    if 0 <= j < ROWS:
                        total[j] = total[j] + value * weight[a]
        write(ct, lanes, total)
        return 0

    lax.fori_loop(0, 3, tile, 0)


def beyond_into(wide, taps, write):
    def tile(ct, _):
        lanes = pl.ds(pl.multiple_of(ct * 128, 128), 128)
        total = [jnp.zeros((COLS, 128), F32) for _ in range(PAD)]
        for b in range(KW):
            for a in range(4, KW):
                tap = a * KW + b
                weight = taps[tap : tap + 1, lanes]
                for j in range(PAD):
                    r = ROWS + j + 6 - a
                    if r <= ROWS + PAD - 1:
                        value = wide[ct, r, 11 - b : 11 - b + COLS, :]
                        total[j] = total[j] + value * weight
        write(lanes, total)
        return 0

    lax.fori_loop(0, 3, tile, 0)


def body(
    state, ghost, cot, ocean, taps_in, gain_in, shift_in, wup_in, bup_in, wdown_in, bdown_in, scale_in,
    gs_out, edge_out, beyond_out, tile_out, gk_out, gc_out, gb_out,
    xs, cs, oc, taps, gain, shift, wup0, bup0, wdown0, bdown, scale,
    hw, he, hv, cw, ce, dw, de, dv, ew, ee,
    wide, dwide, wup, wdown, bup, conv, unit, rstd, normed, masked, dbr, dhid, pre, hidden, dpre, dnorm, dcv, dcb,
    g, gc, h, h1, h2, r2, t, tz, perm,
    s, sc, s1, sx, s2, sy, s3, sz, b1, b2, b3,
    loc, hs, hr, qs, qr, ds, dr, es, er, cs_s, cs_r, f_s, f_r, k_s, k_r, z_s, z_r,
    sa_s, sa_r, sx_s, sx_r, sy_s, sy_r, sz_s, sz_r, gy_s, gy_r, gx_s, gx_r, gc_s, gc_r,
):
    ia, ja = lax.axis_index("ia"), lax.axis_index("ja")
    x, zl, c = ia // 16, lax.rem(ia // 2, 8), lax.rem(ia, 2)
    y, zh = ja // 2, lax.rem(ja, 2)
    z = zh * 8 + zl
    top, bottom = ja == BANDS - 1, ja == 0
    east = {"ia": lax.rem(ia + 1, LANES), "ja": ja}
    west = {"ia": lax.rem(ia + LANES - 1, LANES), "ja": ja}
    north = {"ia": ia, "ja": ja + 1}
    south = {"ia": ia, "ja": ja - 1}

    def remote(src, dst, send, recv, device):
        return pltpu.make_async_remote_copy(
            src_ref=src, dst_ref=dst, send_sem=send, recv_sem=recv,
            device_id=device, device_id_type=pl.DeviceIdType.MESH,
        )

    def peer_x(d):
        return place(lax.rem(x + d, 4), y, z, c)

    def peer_y(d):
        return place(x, lax.rem(y + d, 4), z, c)

    def peer_z(d):
        return place(x, y, lax.rem(z + d, 16), c)

    other = place(x, y, z, 1 - c)

    loads = [
        pltpu.make_async_copy(src, dst, loc.at[i])
        for i, (src, dst) in enumerate(
            [
                (state, xs), (cot, cs), (ocean, oc), (taps_in, taps), (gain_in, gain), (shift_in, shift),
                (wup_in, wup0), (bup_in, bup0), (wdown_in, wdown0), (bdown_in, bdown), (scale_in, scale),
            ]
        )
    ]
    for load in loads:
        load.start()

    barrier = pltpu.get_barrier_semaphore()

    def greet(device):
        pl.semaphore_signal(barrier, inc=1, device_id=device, device_id_type=pl.DeviceIdType.MESH)

    greet(east)
    greet(west)
    greet(other)
    for d in range(1, 4):
        greet(peer_x(d))
        greet(peer_y(d))
    for d in range(1, 16):
        greet(peer_z(d))

    greet({"ia": ia, "ja": lax.rem(ja + 1, BANDS)})
    greet({"ia": ia, "ja": lax.rem(ja + BANDS - 1, BANDS)})
    pl.semaphore_wait(barrier, 26)

    def halo(src, w, e, v, send, recv):
        to_north = remote(src.at[5:8], v.at[0], send.at[0], recv.at[0], north)
        to_south = remote(src.at[0:3], v.at[1], send.at[1], recv.at[1], south)
        to_east = remote(src.at[:, 16:32], w, send.at[2], recv.at[2], east)
        to_west = remote(src.at[:, 0:16], e, send.at[3], recv.at[3], west)

        @pl.when(jnp.logical_not(top))
        def _():
            to_north.start()

        @pl.when(jnp.logical_not(bottom))
        def _():
            to_south.start()

        to_east.start()
        to_west.start()
        return to_north, to_south, to_east, to_west

    def corners(v, w, e, send, recv):
        to_east = remote(v.at[:, :, 16:32], w, send.at[0], recv.at[0], east)
        to_west = remote(v.at[:, :, 0:16], e, send.at[1], recv.at[1], west)
        to_east.start()
        to_west.start()
        return to_east, to_west

    def finish_rows(copies):
        to_north, to_south, _, _ = copies

        @pl.when(jnp.logical_not(top))
        def _():
            to_north.wait_send()
            to_south.wait_recv()

        @pl.when(jnp.logical_not(bottom))
        def _():
            to_south.wait_send()
            to_north.wait_recv()

    def widen(dst, v, centre, w, e, v_w, v_e):
        for ct in range(3):
            lanes = slice(ct * 128, ct * 128 + 128)
            for r in range(ROWS):
                dst[ct, PAD + r, 0:8, :] = w[r, :, lanes].astype(F32)[8:16]
                dst[ct, PAD + r, 40:48, :] = e[r, :, lanes].astype(F32)[0:8]
                if centre is not None:
                    dst[ct, PAD + r, 8:40, :] = centre[r, :, lanes].astype(F32)
            for k in range(2):
                for q in range(PAD):
                    r = q + k * (ROWS + PAD)
                    dst[ct, r, 0:8, :] = v_w[k, q, :, lanes].astype(F32)[8:16]
                    dst[ct, r, 40:48, :] = v_e[k, q, :, lanes].astype(F32)[0:8]
                    dst[ct, r, 8:40, :] = v[k, q, :, lanes].astype(F32)

    first = halo(state, hw, he, hv, hs, hr)

    for load in loads:
        load.wait()

    @pl.when(top)
    def _():
        copy = pltpu.make_async_copy(ghost, hv.at[1], loc.at[11])
        copy.start()
        copy.wait()

    @pl.when(bottom)
    def _():
        hv[0] = jnp.zeros((PAD, COLS, CH), BF16)

    def old(p):
        return (p % 384) // 96 * 192 + (p % 96) // 12 * 24 + p // 384 * 12 + p % 12

    perm[...] = onehot(HID, HID, old)
    wup[...] = dot(wup0[...], perm[...]).astype(BF16)
    wdown[...] = dot(wdown0[...], perm[...]).astype(BF16)
    bup[...] = jnp.sum(dot(split3(bup0[...]), perm[...]), axis=0, keepdims=True)

    eye = (
        lax.broadcasted_iota(jnp.int32, (COLS, COLS), 0)
        == lax.broadcasted_iota(jnp.int32, (COLS, COLS), 1)
    ).astype(F32)

    def mask_row(j, total):
        cells = pl.ds(pl.multiple_of(j * COLS, COLS), COLS)
        sea = jnp.sum(eye * oc[pl.ds(j, 1), :].astype(F32), axis=1, keepdims=True)
        value = cs[j].astype(F32) * sea
        masked[cells, :] = value
        value = value * scale[...]
        dbr[cells, :] = value.astype(BF16)
        return total + sub8(value)

    g_bdown = lax.fori_loop(0, ROWS, mask_row, jnp.zeros((8, CH), F32))
    dhid[...] = dot(dbr[...], wdown[...])

    finish_rows(first)
    second = corners(hv, cw, ce, qs, qr)
    for copy in first[2:]:
        copy.wait()
    for copy in second:
        copy.wait()
    widen(wide, hv, xs, hw, he, cw, ce)

    def put_conv(ct, lanes, total):
        for j in range(ROWS):
            conv[j * COLS : (j + 1) * COLS, lanes] = total[j]

    conv_into(wide, taps, False, put_conv)

    def norm_row(j, _):
        cells = pl.ds(pl.multiple_of(j * COLS, COLS), COLS)
        value = conv[cells, :]
        value = value - jnp.mean(value, axis=1, keepdims=True)
        r = lax.rsqrt(jnp.mean(value * value, axis=1, keepdims=True) + 1e-06)
        value = value * r
        rstd[cells, :] = r
        unit[cells, :] = value
        normed[cells, :] = (value * gain[...] + shift[...]).astype(BF16)
        return 0

    lax.fori_loop(0, ROWS, norm_row, 0)
    pre[...] = dot(normed[...], wup[...])

    def gelu_row(j, totals):
        cells = pl.ds(pl.multiple_of(j * COLS, COLS), COLS)
        done = []
        for k in range(3):
            lanes = slice(k * 256, k * 256 + 256)
            v = pre[cells, lanes] + bup[:, lanes]
            square = v * v
            tanh = jnp.tanh(v * (COEFF + COEFF * CUBIC * square))
            half = 0.5 + 0.5 * tanh
            value = v * half
            slope = half + value * (1.0 - tanh) * (COEFF + 3.0 * CUBIC * COEFF * square)
            hidden[cells, lanes] = value.astype(BF16)
            grad = dhid[cells, lanes] * slope
            dpre[cells, lanes] = grad.astype(BF16)
            done.append(totals[k] + sub8(grad))
        return tuple(done)

    g_bup = lax.fori_loop(
        0, ROWS, gelu_row, tuple(jnp.zeros((8, 256), F32) for _ in range(3))
    )
    g_bup = jnp.concatenate([jnp.sum(v, axis=0, keepdims=True) for v in g_bup], axis=1)

    dnorm[...] = dot(dpre[...], wup[...], (1, 1))

    def back_row(j, totals):
        cells = pl.ds(pl.multiple_of(j * COLS, COLS), COLS)
        u = unit[cells, :]
        grad = dnorm[cells, :]
        product = grad * u
        scaled = grad * gain[...]
        mean_a = jnp.mean(scaled, axis=1, keepdims=True)
        mean_b = jnp.mean(product * gain[...], axis=1, keepdims=True)
        value = (rstd[cells, :] * (scaled - mean_a - u * mean_b)).astype(BF16)
        dcb[j] = value
        value = value.astype(F32)
        for ct in range(3):
            dcv[ct, j] = value[:, ct * 128 : ct * 128 + 128]
        return totals[0] + sub8(product), totals[1] + sub8(grad)

    zero = jnp.zeros((8, CH), F32)
    g_gain, g_shift = lax.fori_loop(0, ROWS, back_row, (zero, zero))

    @pl.when(top)
    def _():
        dv[1] = jnp.zeros((PAD, COLS, CH), BF16)

    @pl.when(bottom)
    def _():
        dv[0] = jnp.zeros((PAD, COLS, CH), BF16)

    third = halo(dcb, dw, de, dv, ds, dr)

    for half in range(2):
        units = slice(half * 384, half * 384 + 384)
        g[0, half] = dot(dpre[:, units], normed[...], (0, 0)).astype(BF16)
        g[1, half] = dot(dbr[...], hidden[:, units], (0, 0)).astype(BF16)
    cross = remote(g.at[:, 1 - c], gc, cs_s.at[0], cs_r.at[0], other)
    cross.start()

    branch = dot(hidden[...], wdown[...], (1, 1)) + bdown[...]
    g_scale = jnp.sum(masked[...] * branch, axis=0, keepdims=True)
    back = jnp.sum(dot(split3(g_bup), perm[...], (1, 1)), axis=0, keepdims=True)
    s[...] = jnp.zeros((64, 512), F32)
    s[49:50, 0:CH] = jnp.sum(g_gain, axis=0, keepdims=True)
    s[50:51, 0:CH] = jnp.sum(g_shift, axis=0, keepdims=True)
    s[51:52, 0:CH] = jnp.sum(g_bdown, axis=0, keepdims=True)
    s[52:53, 0:CH] = g_scale
    s[53:54, 0:CH] = back[:, 0:CH]
    s[54:55, 0:CH] = back[:, CH:HID]

    def tap_tile(ct, _):
        lanes = pl.ds(pl.multiple_of(ct * 128, 128), 128)
        for b in range(KW):
            total = [jnp.zeros((8, 128), F32) for _ in range(KW)]
            for r in range(ROWS + 2 * PAD):
                value = wide[ct, r, 5 + b : 5 + b + COLS, :]
                for a in range(KW):
                    j = r - a
                    if 0 <= j < ROWS:
                        total[a] = total[a] + sub8(value * dcv[ct, j])
            for a in range(KW):
                s[a * KW + b : a * KW + b + 1, lanes] = jnp.sum(total[a], axis=0, keepdims=True)
        return 0

    lax.fori_loop(0, 3, tap_tile, 0)

    half_s = pl.multiple_of((1 - c) * 32, 32)
    cross_s = remote(s.at[pl.ds(half_s, 32)], sc, sa_s.at[0], sa_r.at[0], other)
    cross_s.start()

    finish_rows(third)
    fourth = corners(dv, ew, ee, es, er)

    cross.wait()
    for k in range(2):
        for q in range(4):
            rows = slice(q * 96, q * 96 + 96)
            h[k, q] = (g[k, c, rows, :].astype(F32) + gc[k, rows, :].astype(F32)).astype(BF16)
    along = []
    for d in range(1, 4):
        up = remote(h.at[0, lax.rem(x + d, 4)], h1.at[0, d - 1], f_s.at[0, d - 1], f_r.at[0, d - 1], peer_x(d))
        down = remote(h.at[1, lax.rem(y + d, 4)], h1.at[1, d - 1], f_s.at[1, d - 1], f_r.at[1, d - 1], peer_y(d))
        up.start()
        down.start()
        along += [up, down]

    cross_s.wait()
    mine_s = pl.multiple_of(c * 32, 32)
    s1[...] = (s[pl.ds(mine_s, 32), :] + sc[...]).reshape(4, 8, 512)
    small = []
    for d in range(1, 4):
        copy = remote(s1.at[lax.rem(x + d, 4)], sx.at[d - 1], sx_s.at[d - 1], sx_r.at[d - 1], peer_x(d))
        copy.start()
        small.append(copy)

    for copy in third[2:]:
        copy.wait()
    for copy in fourth:
        copy.wait()
    widen(dwide, dv, dcb, dw, de, ew, ee)

    def put_back(ct, lanes, total):
        for j in range(ROWS):
            value = cs[j, :, lanes].astype(F32) + total[j]
            gs_out[j, :, lanes] = value.astype(BF16)
            if 4 <= j < 7:
                edge_out[j - 4, :, lanes] = value

    conv_into(dwide, taps, True, put_back)

    def put_beyond(lanes, total):
        for j in range(PAD):
            beyond_out[j, :, lanes] = total[j].astype(BF16)

    beyond_into(dwide, taps, put_beyond)

    for copy in small:
        copy.wait()
    s2[...] = s1[x] + sx[0] + sx[1] + sx[2]
    small = []
    for d in range(1, 4):
        chunk = pl.ds(pl.multiple_of(lax.rem(y + d, 4) * 128, 128), 128)
        copy = remote(s2.at[:, chunk], sy.at[d - 1], sy_s.at[d - 1], sy_r.at[d - 1], peer_y(d))
        copy.start()
        small.append(copy)

    for copy in along:
        copy.wait()
    spread = onehot(CH, 512, lambda p: jnp.where(p % 128 < 96, p // 128 * 96 + p % 128, -1))
    for k in range(2):
        mine = h[k, (x, y)[k]].astype(F32)
        mine = mine + h1[k, 0].astype(F32) + h1[k, 1].astype(F32) + h1[k, 2].astype(F32)
        mine = dot(mine.astype(BF16), spread).astype(BF16)
        for q in range(4):
            h2[k, q] = mine[:, q * 128 : q * 128 + 128]
    along = []
    for d in range(1, 4):
        up = remote(h2.at[0, lax.rem(y + d, 4)], r2.at[0, d - 1], k_s.at[0, d - 1], k_r.at[0, d - 1], peer_y(d))
        down = remote(h2.at[1, lax.rem(x + d, 4)], r2.at[1, d - 1], k_s.at[1, d - 1], k_r.at[1, d - 1], peer_x(d))
        up.start()
        down.start()
        along += [up, down]

    for copy in small:
        copy.wait()
    mine_y = pl.ds(pl.multiple_of(y * 128, 128), 128)
    s3[...] = s2[:, mine_y] + sy[0] + sy[1] + sy[2]
    small = []
    for d in range(1, 16):
        copy = remote(s3, sz.at[z], sz_s.at[d - 1], sz_r.at[d - 1], peer_z(d))
        copy.start()
        small.append(copy)

    for copy in along:
        copy.wait()
    parts = []
    for k in range(2):
        mine = h2[k, (y, x)[k]].astype(F32)
        mine = mine + r2[k, 0].astype(F32) + r2[k, 1].astype(F32) + r2[k, 2].astype(F32)
        parts.append(mine.astype(BF16))
    pick_up = onehot(128, 256, lambda p: jnp.where(p % 128 < 48, p // 128 * 48 + p % 128, -1))
    pick_down = onehot(
        96, 256, lambda p: jnp.where((p % 128 >= 64) & (p % 128 < 112), p // 128 * 48 + p % 128 - 64, -1)
    )
    both = dot(parts[0], pick_up) + dot(parts[1], pick_down, (0, 0))[0:96]
    rows_to = onehot(96, 128, lambda p: jnp.where(p % 16 < 12, p // 16 * 12 + p % 16, -1))
    tiles = dot(rows_to, both.astype(BF16), (0, 0)).astype(BF16)
    for q in range(16):
        t[q] = tiles[q % 8 * 16 : q % 8 * 16 + 16, q // 8 * 128 : q // 8 * 128 + 128]
    along = []
    for d in range(1, 16):
        copy = remote(t.at[lax.rem(z + d, 16)], tz.at[d - 1], z_s.at[d - 1], z_r.at[d - 1], peer_z(d))
        copy.start()
        along.append(copy)

    sz[z] = s3[...]
    for copy in small:
        copy.wait()
    total = sz[0]
    for q in range(1, 16):
        total = total + sz[q]
    b1[:, mine_y] = total * FACTOR
    gather = []
    for d in range(1, 4):
        copy = remote(b1.at[:, mine_y], b1.at[:, mine_y], gy_s.at[d - 1], gy_r.at[d - 1], peer_y(d))
        copy.start()
        gather.append(copy)
    for copy in gather:
        copy.wait()
    b2[x] = b1[...]
    gather = []
    for d in range(1, 4):
        copy = remote(b1, b2.at[x], gx_s.at[d - 1], gx_r.at[d - 1], peer_x(d))
        copy.start()
        gather.append(copy)
    for copy in gather:
        copy.wait()
    b3[c] = b2[...]
    copy = remote(b2, b3.at[c], gc_s.at[0], gc_r.at[0], other)
    copy.start()
    copy.wait()
    final = b3[...].reshape(64, 512)
    gk_out[...] = final[0:49, 0:CH]
    gc_out[...] = final[49:53, 0:CH]
    gb_out[...] = final[53:55, 0:CH]

    for copy in along:
        copy.wait()
    total = t[z].astype(F32)
    for d in range(15):
        total = total + tz[d].astype(F32)
    tile_out[...] = total * FACTOR


def fused(state, ghost, cot, ocean, taps, gain, shift, wup, bup, wdown, bdown, scale):
    sds = jax.ShapeDtypeStruct
    vm = pltpu.VMEM
    dma = pltpu.SemaphoreType.DMA
    any_spec = pl.BlockSpec(memory_space=pl.ANY)
    vm_spec = pl.BlockSpec(memory_space=pltpu.VMEM)
    edge16 = (ROWS, 16, CH)
    corner = (2, PAD, 16, CH)
    scratch = [
        vm((ROWS, COLS, CH), BF16), vm((ROWS, COLS, CH), BF16), vm((ROWS, COLS), jnp.int32),
        vm((49, CH), F32), vm((1, CH), F32), vm((1, CH), F32), vm((CH, HID), BF16), vm((1, HID), F32),
        vm((CH, HID), BF16), vm((1, CH), F32), vm((1, CH), F32),
        vm(edge16, BF16), vm(edge16, BF16), vm((2, PAD, COLS, CH), BF16), vm(corner, BF16), vm(corner, BF16),
        vm(edge16, BF16), vm(edge16, BF16), vm((2, PAD, COLS, CH), BF16), vm(corner, BF16), vm(corner, BF16),
        vm((3, 14, WIDE, 128), F32), vm((3, 14, WIDE, 128), F32),
        vm((CH, HID), BF16), vm((CH, HID), BF16), vm((1, HID), F32),
        vm((CELLS, CH), F32), vm((CELLS, CH), F32), vm((CELLS, 1), F32), vm((CELLS, CH), BF16),
        vm((CELLS, CH), F32), vm((CELLS, CH), BF16), vm((CELLS, HID), F32), vm((CELLS, HID), F32),
        vm((CELLS, HID), BF16), vm((CELLS, HID), BF16), vm((CELLS, CH), F32),
        vm((3, ROWS, COLS, 128), F32), vm((ROWS, COLS, CH), BF16),
        vm((2, 2, 384, 384), BF16), vm((2, 384, 384), BF16), vm((2, 4, 96, 384), BF16),
        vm((2, 3, 96, 384), BF16), vm((2, 4, 96, 128), BF16), vm((2, 3, 96, 128), BF16),
        vm((16, 16, 128), BF16), vm((15, 16, 128), BF16), vm((HID, HID), BF16),
        vm((64, 512), F32), vm((32, 512), F32), vm((4, 8, 512), F32), vm((3, 8, 512), F32), vm((8, 512), F32),
        vm((3, 8, 128), F32), vm((8, 128), F32), vm((16, 8, 128), F32), vm((8, 512), F32), vm((4, 8, 512), F32),
        vm((2, 4, 8, 512), F32),
        dma((12,)), dma((4,)), dma((4,)), dma((2,)), dma((2,)), dma((4,)), dma((4,)), dma((2,)), dma((2,)),
        dma((1,)), dma((1,)), dma((2, 3)), dma((2, 3)), dma((2, 3)), dma((2, 3)), dma((15,)), dma((15,)),
        dma((1,)), dma((1,)), dma((3,)), dma((3,)), dma((3,)), dma((3,)), dma((15,)), dma((15,)),
        dma((3,)), dma((3,)), dma((3,)), dma((3,)), dma((1,)), dma((1,)),
    ]
    return pl.pallas_call(
        body,
        out_shape=[
            sds((ROWS, COLS, CH), BF16), sds((PAD, COLS, CH), F32), sds((PAD, COLS, CH), BF16),
            sds((16, 128), F32), sds((49, CH), F32), sds((4, CH), F32), sds((2, CH), F32),
        ],
        in_specs=[any_spec] * 12,
        out_specs=[vm_spec] * 7,
        scratch_shapes=scratch,
        compiler_params=pltpu.CompilerParams(
            collective_id=0, has_side_effects=True, vmem_limit_bytes=50 * 2**20
        ),
        name="block",
    )(state, ghost, cot, ocean, taps, gain, shift, wup, bup, wdown, bdown, scale)


def across(strip, partner):
    pivot = lax.rem(partner + lax.axis_index("ia"), LANES)

    def branch(k):
        pairs = [
            (a * BANDS + BANDS - 1, (k - a) % LANES * BANDS + BANDS - 1) for a in range(LANES)
        ]
        return lambda v: lax.ppermute(v, ("ia", "ja"), pairs)

    return lax.switch(pivot, [branch(k) for k in range(LANES)], strip)[::-1, ::-1]


def local(
    state, cotangent, ocean, fold_partner, kernel, ln_gain, ln_shift, w_up, b_up, w_down, b_down, layer_scale
):
    on_top = lax.axis_index("ja") == BANDS - 1
    ghost = across(state[4:7], fold_partner[0])
    gs, edge, beyond, tile, g_kernel, g_chan, g_bup = fused(
        state, ghost, cotangent, ocean, kernel, ln_gain[None], ln_shift[None], w_up, b_up[None],
        w_down, b_down[None], layer_scale[None],
    )
    fold = across(beyond, fold_partner[0])
    edge = edge + jnp.where(on_top, fold.astype(F32), 0.0)
    grad_state = jnp.concatenate([gs[0:4], edge.astype(BF16), gs[7:8]], axis=0)
    grad_up = tile[0:12, 0:48].T
    grad_down = tile[0:12, 64:112].T
    return grad_state, grad_up, grad_down, g_kernel, g_chan, g_bup.reshape(HID)


def solution(mesh):
    placed = (P("ja", "ia", None), P("ja", "ia", None), P("ja", "ia"), P("ia")) + (P(),) * 8
    return jax.shard_map(
        local,
        mesh=mesh,
        in_specs=placed,
        out_specs=(P("ja", "ia", None), P("ja", "ia"), P("ja", "ia"), P(), P(), P()),
        check_vma=False,
    )
```

```python
import functools
import math

import jax
import jax.numpy as jnp
from jax import lax
from jax.experimental import pallas as pl
from jax.experimental.pallas import tpu as pltpu
from jax.sharding import PartitionSpec as P

KW = 7
PAD = 3
ROWS = 8
COLS = 32
CH = 384
HID = 768
CELLS = ROWS * COLS
WIDE = 48
F32 = jnp.float32
BF16 = jnp.bfloat16
LANES = 64
BANDS = 8
COEFF = 0.7978845608028654
CUBIC = 0.044715
FACTOR = 1.0 / math.sqrt(ROWS * BANDS * COLS * LANES)


def place(x, y, z, c):
    return {"ia": x * 16 + lax.rem(z, 8) * 2 + c, "ja": y * 2 + z // 8}


def dot(a, b, dims=(1, 0)):
    return lax.dot_general(
        a, b, (((dims[0],), (dims[1],)), ((), ())), preferred_element_type=F32
    )


def sub8(v):
    return v[0:8] + v[8:16] + v[16:24] + v[24:32]


def onehot(rows, cols, target):
    want = target(lax.broadcasted_iota(jnp.int32, (1, cols), 1))
    here = lax.broadcasted_iota(jnp.int32, (rows, cols), 0)
    return jnp.where(here == want, 1.0, 0.0).astype(BF16)


def split3(v):
    hi = v.astype(BF16)
    rest = v - hi.astype(F32)
    mid = rest.astype(BF16)
    low = (rest - mid.astype(F32)).astype(BF16)
    zeros = jnp.zeros((13, v.shape[1]), F32)
    return jnp.concatenate(
        [hi.astype(F32), mid.astype(F32), low.astype(F32), zeros], axis=0
    ).astype(BF16)


def conv_part(wide, taps, flip, rows, spans, read, write):
    def tile(ct, _):
        lanes = pl.ds(pl.multiple_of(ct * 128, 128), 128)
        for start, width in spans:
            hit = [j for j in range(ROWS) if any(0 <= r - j < KW for r in rows)]
            total = {j: read(ct, j, start, width) for j in hit}
            for b in range(KW):
                weight = []
                for a in range(KW):
                    tap = a * KW + b
                    tap = KW * KW - 1 - tap if flip else tap
                    weight.append(taps[tap : tap + 1, lanes])
                for r in rows:
                    value = wide[ct, r, 5 + b + start : 5 + b + start + width, :]
                    for a in range(KW):
                        if r - a in total:
                            total[r - a] = total[r - a] + value * weight[a]
            for j in hit:
                write(ct, lanes, j, start, width, total[j])
        return 0

    lax.fori_loop(0, 3, tile, 0)


def fold_into(edge, taps, read, write):
    def tile(ct, _):
        lanes = pl.ds(pl.multiple_of(ct * 128, 128), 128)
        total = [read(j, lanes) for j in range(3)]
        for b in range(KW):
            for j in range(3):
                for e in range(j + 1):
                    a = e + 6 - j
                    weight = taps[a * KW + b : a * KW + b + 1, lanes]
                    total[j] = total[j] + edge[ct, e, 5 + b : 5 + b + COLS, :] * weight
        for j in range(3):
            write(j, lanes, total[j])
        return 0

    lax.fori_loop(0, 3, tile, 0)


def fold_slots(p):
    q = jnp.where(p < 112, p - 96, p - 112)
    first = q // 3 * COLS + q % 3
    edge = jnp.where(q < 9, jnp.where(p < 112, first, first + COLS - 3), -1)
    return jnp.where(p < 96, p, edge)


def fold_cells(p):
    row, col = p // WIDE, p % WIDE
    west = 96 + (2 - row) * 3 + 7 - col
    east = 112 + (2 - row) * 3 + 42 - col
    inner = 95 - row * COLS - (col - 8)
    slot = jnp.where(col < 8, west, jnp.where(col < 40, inner, east))
    return jnp.where((col >= 5) & (col < 43), slot, -1)


def fold_swap(p):
    return p % 16 // 2 * 16 + p // 16 * 2 + p % 2


def body(
    state, cot, ocean, partner, taps_in, gain_in, shift_in, wup_in, bup_in, wdown_in, bdown_in, scale_in,
    gs_out, tile_out, small_out,
    xs, cs, oc, part, taps, gain, shift, wup0, bup0, wdown0, bdown, scale,
    hw, he, hv, cw, ce, dw, de, dv, ew, ee,
    wide, dwide, edge, acc, bacc, edge_rows, wup, wdown, bup,
    unit, rstd, normed, masked, dbr, dhid, pre, hidden, dpre, dnorm, dcv, dcb,
    g, gc, h, h1, h2, r2, t, tz, perm,
    s, sc, s1, sx, s2, sy, s3, sz, b1, b2, b3, fold,
    loc, hs, hr, qs, qr, ds, dr, es, er, cs_s, cs_r, f_s, f_r, k_s, k_r, z_s, z_r,
    sa_s, sa_r, sx_s, sx_r, sy_s, sy_r, sz_s, sz_r, gy_s, gy_r, gx_s, gx_r, gc_s, gc_r, fold_s, fold_r,
):
    ia, ja = lax.axis_index("ia"), lax.axis_index("ja")
    x, zl, c = ia // 16, lax.rem(ia // 2, 8), lax.rem(ia, 2)
    y, zh = ja // 2, lax.rem(ja, 2)
    z = zh * 8 + zl
    u = x * 2 + c
    top, bottom = ja == BANDS - 1, ja == 0
    east = {"ia": lax.rem(ia + 1, LANES), "ja": ja}
    west = {"ia": lax.rem(ia + LANES - 1, LANES), "ja": ja}
    north = {"ia": ia, "ja": ja + 1}
    south = {"ia": ia, "ja": ja - 1}

    def remote(src, dst, send, recv, device):
        return pltpu.make_async_remote_copy(
            src_ref=src, dst_ref=dst, send_sem=send, recv_sem=recv,
            device_id=device, device_id_type=pl.DeviceIdType.MESH,
        )

    def peer_x(d):
        return place(lax.rem(x + d, 4), y, z, c)

    def peer_y(d):
        return place(x, lax.rem(y + d, 4), z, c)

    def peer_z(d):
        return place(x, y, lax.rem(z + d, 16), c)

    def peer_u(d):
        to = lax.rem(u + d, 8)
        return {"ia": to // 2 * 16 + zl * 2 + lax.rem(to, 2), "ja": ja}

    def peer_v(d):
        return {"ia": x * 16 + lax.rem(zl + d, 8) * 2 + c, "ja": ja}

    other = place(x, y, z, 1 - c)

    loads = [
        pltpu.make_async_copy(src, dst, loc.at[i])
        for i, (src, dst) in enumerate(
            [
                (state, xs), (cot, cs), (ocean, oc), (taps_in, taps), (gain_in, gain), (shift_in, shift),
                (wup_in, wup0), (bup_in, bup0), (wdown_in, wdown0), (bdown_in, bdown), (scale_in, scale),
                (partner, part),
            ]
        )
    ]
    for load in loads:
        load.start()

    barrier = pltpu.get_barrier_semaphore()

    def greet(device):
        pl.semaphore_signal(barrier, inc=1, device_id=device, device_id_type=pl.DeviceIdType.MESH)

    greet({"ia": ia, "ja": lax.rem(ja + 1, BANDS)})
    greet({"ia": ia, "ja": lax.rem(ja + BANDS - 1, BANDS)})
    greet(east)
    greet(west)

    @pl.when(top)
    def _():
        for d in range(1, 8):
            greet(peer_u(d))
            greet(peer_v(d))

    for d in range(1, 16):
        greet(peer_z(d))
    for d in range(1, 4):
        greet(peer_x(d))
        greet(peer_y(d))
    greet(other)

    for load in loads:
        load.wait()

    def old(p):
        return (p % 384) // 96 * 192 + (p % 96) // 12 * 24 + p // 384 * 12 + p % 12

    perm[...] = onehot(HID, HID, old)
    wup[...] = dot(wup0[...], perm[...]).astype(BF16)
    wdown[...] = dot(wdown0[...], perm[...]).astype(BF16)
    bup[...] = jnp.sum(dot(split3(bup0[...][None]), perm[...]), axis=0, keepdims=True)

    eye = (
        lax.broadcasted_iota(jnp.int32, (COLS, COLS), 0)
        == lax.broadcasted_iota(jnp.int32, (COLS, COLS), 1)
    ).astype(F32)

    def mask_row(j, total):
        sea = jnp.sum(eye * oc[pl.ds(j, 1), :].astype(F32), axis=1, keepdims=True)
        value = cs[j].astype(F32) * sea
        halves = (value[8:24], jnp.concatenate([value[0:8], value[24:32]], axis=0))
        for k in range(2):
            cells = pl.ds(pl.multiple_of(k * 128 + j * 16, 16), 16)
            masked[cells, :] = halves[k]
            dbr[cells, :] = (halves[k] * scale[...][None]).astype(BF16)
        return total + sub8(value * scale[...][None])

    g_bdown = lax.fori_loop(0, ROWS, mask_row, jnp.zeros((8, CH), F32))
    dhid[...] = dot(dbr[...], wdown[...])

    def widen_own(dst, centre):
        for ct in range(3):
            lanes = slice(ct * 128, ct * 128 + 128)
            for r in range(ROWS):
                dst[ct, PAD + r, 8:40, :] = centre[r, :, lanes].astype(F32)

    def widen_sides(dst, w, e):
        for ct in range(3):
            lanes = slice(ct * 128, ct * 128 + 128)
            for r in range(ROWS):
                dst[ct, PAD + r, 0:8, :] = w[r, :, lanes].astype(F32)[8:16]
                dst[ct, PAD + r, 40:48, :] = e[r, :, lanes].astype(F32)[0:8]

    def widen_rows(dst, v, k):
        for ct in range(3):
            lanes = slice(ct * 128, ct * 128 + 128)
            for q in range(PAD):
                dst[ct, q + k * (ROWS + PAD), 8:40, :] = v[k, q, :, lanes].astype(F32)

    def widen_corners(dst, w, e, k):
        for ct in range(3):
            lanes = slice(ct * 128, ct * 128 + 128)
            for q in range(PAD):
                dst[ct, q + k * (ROWS + PAD), 0:8, :] = w[k, q, :, lanes].astype(F32)[8:16]
                dst[ct, q + k * (ROWS + PAD), 40:48, :] = e[k, q, :, lanes].astype(F32)[0:8]

    widen_own(wide, xs)

    pl.semaphore_wait(barrier, 26 + jnp.where(top, 14, 0))

    def halo(src, w, e, v, send, recv):
        to_north = remote(src.at[5:8], v.at[0], send.at[0], recv.at[0], north)
        to_south = remote(src.at[0:3], v.at[1], send.at[1], recv.at[1], south)
        to_east = remote(src.at[:, 16:32], w, send.at[2], recv.at[2], east)
        to_west = remote(src.at[:, 0:16], e, send.at[3], recv.at[3], west)

        @pl.when(jnp.logical_not(top))
        def _():
            to_north.start()

        @pl.when(jnp.logical_not(bottom))
        def _():
            to_south.start()

        to_east.start()
        to_west.start()
        return to_north, to_south, to_east, to_west

    def finish_rows(copies):
        to_north, to_south, _, _ = copies

        @pl.when(jnp.logical_not(top))
        def _():
            to_north.wait_send()
            to_south.wait_recv()

        @pl.when(jnp.logical_not(bottom))
        def _():
            to_south.wait_send()
            to_north.wait_recv()

    def corners(v, w, e, send, recv):
        copies = []
        for k in range(2):
            copies.append(remote(v.at[k, :, 16:32], w.at[k], send.at[2 * k], recv.at[2 * k], east))
            copies.append(remote(v.at[k, :, 0:16], e.at[k], send.at[2 * k + 1], recv.at[2 * k + 1], west))
        copies[0].start()
        copies[1].start()

        @pl.when(jnp.logical_not(top))
        def _():
            copies[2].start()
            copies[3].start()

        return copies

    def finish_corners(dst, copies, w, e):
        copies[0].wait()
        copies[1].wait()
        widen_corners(dst, w, e, 0)

        @pl.when(jnp.logical_not(top))
        def _():
            copies[2].wait()
            copies[3].wait()
            widen_corners(dst, w, e, 1)

    def fold_copies(k, step, peer, me):
        return [
            remote(
                fold.at[k, step, 0, lax.rem(me + d, 8)], fold.at[k, step, 1, me],
                fold_s.at[k, step, d - 1], fold_r.at[k, step, d - 1], peer(d),
            )
            for d in range(1, 8)
        ]

    fold_steps = ((peer_u, u), (peer_v, zl), (peer_v, zl), (peer_u, u))

    def fold_send(k, step, value):
        peer, me = fold_steps[step]
        fold[k, step, 0] = value.astype(BF16).reshape(8, 16, CH)
        for copy in fold_copies(k, step, peer, me):
            copy.start()
        fold[k, step, 1, me] = fold[k, step, 0, me]

    def fold_take(k, step):
        peer, me = fold_steps[step]
        for copy in fold_copies(k, step, peer, me):
            copy.wait()
        return fold[k, step, 1].reshape(128, CH)

    def fold_first(k, strip):
        fold_send(k, 0, dot(onehot(96, 128, fold_slots), strip, (0, 0)))

    def fold_next(k, step):
        value = fold_take(k, step - 1)

        def facing(p):
            into = p % 16 // 2
            target = into // 2 * 16 + p // 16 * 2 + into % 2
            shift = jnp.where(u == 6, 1, 0) - jnp.where(u == 7, 1, 0)
            source = (part[...] + ia - target + shift + LANES) % LANES
            return source // 2 % 8 * 16 + (source // 16 * 2 + source % 2) * 2 + p % 2

        matrix = onehot(128, 128, facing if step == 2 else fold_swap)
        fold_send(k, step, dot(matrix, value, (0, 0)))

    def fold_last(k):
        return dot(onehot(128, PAD * WIDE, fold_cells), fold_take(k, 3), (0, 0))

    first = halo(state, hw, he, hv, hs, hr)

    @pl.when(top)
    def _():
        fold_first(0, xs[4:7].reshape(96, CH))

    @pl.when(bottom)
    def _():
        hv[0] = jnp.zeros((PAD, COLS, CH), BF16)

    middle, sides = ((8, 16),), ((0, 8), (24, 8))
    own, beyond = tuple(range(PAD, PAD + ROWS)), (0, 1, 2, 11, 12, 13)

    def nothing(ct, j, start, width):
        return jnp.zeros((width, 128), F32)

    def read_acc(ct, j, start, width):
        return acc[ct, j, start : start + width, :]

    def write_acc(ct, lanes, j, start, width, value):
        acc[ct, j, start : start + width, :] = value

    conv_part(wide, taps, False, own, middle, nothing, write_acc)
    for copy in first[2:]:
        copy.wait()
    widen_sides(wide, hw, he)

    @pl.when(top)
    def _():
        fold_next(0, 1)

    conv_part(wide, taps, False, own, sides, nothing, write_acc)

    @pl.when(top)
    def _():
        fold_next(0, 2)
        fold_next(0, 3)

    finish_rows(first)
    second = corners(hv, cw, ce, qs, qr)
    widen_rows(wide, hv, 0)

    @pl.when(jnp.logical_not(top))
    def _():
        widen_rows(wide, hv, 1)

    @pl.when(top)
    def _():
        ghost = fold_last(0)
        for ct in range(3):
            for q in range(PAD):
                wide[ct, ROWS + PAD + q] = ghost[q * WIDE : (q + 1) * WIDE, ct * 128 : ct * 128 + 128]

    def half_pass(k):
        base = k * 128
        block = slice(base, base + 128)
        spans = (middle, sides)[k]
        conv_part(wide, taps, False, beyond, spans, read_acc, write_acc)

        def norm_rows(i, _):
            cells = pl.ds(pl.multiple_of(base + i * 32, 32), 32)
            value = jnp.concatenate(
                [
                    jnp.concatenate(
                        [acc[ct, 2 * i + q, start : start + width, :] for q in range(2) for start, width in spans],
                        axis=0,
                    )
                    for ct in range(3)
                ],
                axis=1,
            )
            value = value - jnp.mean(value, axis=1, keepdims=True)
            r = lax.rsqrt(jnp.mean(value * value, axis=1, keepdims=True) + 1e-06)
            value = value * r
            rstd[cells, :] = r
            unit[cells, :] = value
            normed[cells, :] = (value * gain[...][None] + shift[...][None]).astype(BF16)
            return 0

        lax.fori_loop(0, 4, norm_rows, 0)
        pre[...] = dot(normed[block, :], wup[...])

        def gelu_rows(i, totals):
            here = pl.ds(pl.multiple_of(i * 32, 32), 32)
            cells = pl.ds(pl.multiple_of(base + i * 32, 32), 32)
            done = []
            for q in range(3):
                lanes = slice(q * 256, q * 256 + 256)
                v = pre[here, lanes] + bup[:, lanes]
                square = v * v
                tanh = jnp.tanh(v * (COEFF + COEFF * CUBIC * square))
                half = 0.5 + 0.5 * tanh
                value = v * half
                slope = half + value * (1.0 - tanh) * (COEFF + 3.0 * CUBIC * COEFF * square)
                hidden[cells, lanes] = value.astype(BF16)
                grad = dhid[cells, lanes] * slope
                dpre[cells, lanes] = grad.astype(BF16)
                done.append(totals[q] + sub8(grad))
            return tuple(done)

        bias = lax.fori_loop(0, 4, gelu_rows, tuple(jnp.zeros((8, 256), F32) for _ in range(3)))
        dnorm[...] = dot(dpre[block, :], wup[...], (1, 1))

        def back_rows(i, totals):
            here = pl.ds(pl.multiple_of(i * 32, 32), 32)
            cells = pl.ds(pl.multiple_of(base + i * 32, 32), 32)
            unit_rows = unit[cells, :]
            grad = dnorm[here, :]
            product = grad * unit_rows
            scaled = grad * gain[...][None]
            mean_a = jnp.mean(scaled, axis=1, keepdims=True)
            mean_b = jnp.mean(product * gain[...][None], axis=1, keepdims=True)
            value = rstd[cells, :] * (scaled - mean_a - unit_rows * mean_b)
            value = value.astype(BF16).astype(F32)
            for ct in range(3):
                lanes = slice(ct * 128, ct * 128 + 128)
                at = 0
                for q in range(2):
                    for start, width in spans:
                        dcv[ct, 2 * i + q, start : start + width, :] = value[at : at + width, lanes]
                        at += width
            return totals[0] + sub8(product), totals[1] + sub8(grad)

        zero = jnp.zeros((8, CH), F32)
        return bias, lax.fori_loop(0, 4, back_rows, (zero, zero))

    bias_a, norm_a = half_pass(0)

    finish_corners(wide, second, cw, ce)
    bias_b, norm_b = half_pass(1)

    for ct in range(3):
        for r in range(ROWS):
            dcb[r, :, ct * 128 : ct * 128 + 128] = dcv[ct, r].astype(BF16)

    @pl.when(bottom)
    def _():
        dv[0] = jnp.zeros((PAD, COLS, CH), BF16)

    third = halo(dcb, dw, de, dv, ds, dr)

    @pl.when(top)
    def _():
        fold_first(1, dcb[5:8].reshape(96, CH))

    for half in range(2):
        units = slice(half * 384, half * 384 + 384)
        g[0, half] = dot(dpre[:, units], normed[...], (0, 0)).astype(BF16)
        g[1, half] = dot(dbr[...], hidden[:, units], (0, 0)).astype(BF16)
    cross = remote(g.at[:, 1 - c], gc, cs_s.at[0], cs_r.at[0], other)
    cross.start()

    def tap_tile(ct, _):
        lanes = pl.ds(pl.multiple_of(ct * 128, 128), 128)
        for b in range(KW):
            total = [jnp.zeros((8, 128), F32) for _ in range(KW)]
            for r in range(ROWS + 2 * PAD):
                value = wide[ct, r, 5 + b : 5 + b + COLS, :]
                for a in range(KW):
                    j = r - a
                    if 0 <= j < ROWS:
                        total[a] = total[a] + sub8(value * dcv[ct, j])
            for a in range(KW):
                s[a * KW + b : a * KW + b + 1, lanes] = jnp.sum(total[a], axis=0, keepdims=True)
        return 0

    s[...] = jnp.zeros((64, 512), F32)
    lax.fori_loop(0, 3, tap_tile, 0)

    branch = dot(hidden[...], wdown[...], (1, 1)) + bdown[...][None]
    g_scale = jnp.sum(masked[...] * branch, axis=0, keepdims=True)
    g_bup = jnp.concatenate(
        [jnp.sum(va + vb, axis=0, keepdims=True) for va, vb in zip(bias_a, bias_b)], axis=1
    )
    back = jnp.sum(dot(split3(g_bup), perm[...], (1, 1)), axis=0, keepdims=True)
    s[49:50, 0:CH] = jnp.sum(norm_a[0] + norm_b[0], axis=0, keepdims=True)
    s[50:51, 0:CH] = jnp.sum(norm_a[1] + norm_b[1], axis=0, keepdims=True)
    s[51:52, 0:CH] = jnp.sum(g_bdown, axis=0, keepdims=True)
    s[52:53, 0:CH] = g_scale
    s[53:54, 0:CH] = back[:, 0:CH]
    s[54:55, 0:CH] = back[:, CH:HID]
    half_s = pl.multiple_of((1 - c) * 32, 32)
    cross_s = remote(s.at[pl.ds(half_s, 32)], sc, sa_s.at[0], sa_r.at[0], other)
    cross_s.start()

    cross.wait()
    for k in range(2):
        for q in range(4):
            rows = slice(q * 96, q * 96 + 96)
            h[k, q] = (g[k, c, rows, :].astype(F32) + gc[k, rows, :].astype(F32)).astype(BF16)
    along = []
    for d in range(1, 4):
        up = remote(h.at[0, lax.rem(x + d, 4)], h1.at[0, d - 1], f_s.at[0, d - 1], f_r.at[0, d - 1], peer_x(d))
        down = remote(h.at[1, lax.rem(y + d, 4)], h1.at[1, d - 1], f_s.at[1, d - 1], f_r.at[1, d - 1], peer_y(d))
        up.start()
        down.start()
        along += [up, down]

    cross_s.wait()
    mine_s = pl.multiple_of(c * 32, 32)
    s1[...] = (s[pl.ds(mine_s, 32), :] + sc[...]).reshape(4, 8, 512)
    small = []
    for d in range(1, 4):
        copy = remote(s1.at[lax.rem(x + d, 4)], sx.at[d - 1], sx_s.at[d - 1], sx_r.at[d - 1], peer_x(d))
        copy.start()
        small.append(copy)

    @pl.when(top)
    def _():
        fold_next(1, 1)

    def read_bacc(ct, j, start, width):
        return bacc[ct, j, start : start + width, :]

    def put_back(ct, lanes, j, start, width, value):
        value = cs[j, :, lanes].astype(F32) + value
        gs_out[j, :, lanes] = value.astype(BF16)
        if 4 <= j < 7:
            edge_rows[j - 4, :, lanes] = value

    def write_bacc(ct, lanes, j, start, width, value):
        if 3 <= j < 5:
            put_back(ct, lanes, j, start, width, value)
        else:
            bacc[ct, j, start : start + width, :] = value

    widen_own(dwide, dcb)
    for copy in third[2:]:
        copy.wait()
    widen_sides(dwide, dw, de)
    conv_part(dwide, taps, True, own, ((0, COLS),), nothing, write_bacc)

    for copy in small:
        copy.wait()
    s2[...] = s1[x] + sx[0] + sx[1] + sx[2]
    small = []
    for d in range(1, 4):
        chunk = pl.ds(pl.multiple_of(lax.rem(y + d, 4) * 128, 128), 128)
        copy = remote(s2.at[:, chunk], sy.at[d - 1], sy_s.at[d - 1], sy_r.at[d - 1], peer_y(d))
        copy.start()
        small.append(copy)

    for copy in along:
        copy.wait()
    spread = onehot(CH, 512, lambda p: jnp.where(p % 128 < 96, p // 128 * 96 + p % 128, -1))
    for k in range(2):
        mine = h[k, (x, y)[k]].astype(F32)
        mine = mine + h1[k, 0].astype(F32) + h1[k, 1].astype(F32) + h1[k, 2].astype(F32)
        mine = dot(mine.astype(BF16), spread).astype(BF16)
        for q in range(4):
            h2[k, q] = mine[:, q * 128 : q * 128 + 128]
    along = []
    for d in range(1, 4):
        up = remote(h2.at[0, lax.rem(y + d, 4)], r2.at[0, d - 1], k_s.at[0, d - 1], k_r.at[0, d - 1], peer_y(d))
        down = remote(h2.at[1, lax.rem(x + d, 4)], r2.at[1, d - 1], k_s.at[1, d - 1], k_r.at[1, d - 1], peer_x(d))
        up.start()
        down.start()
        along += [up, down]

    for copy in small:
        copy.wait()
    mine_y = pl.ds(pl.multiple_of(y * 128, 128), 128)
    s3[...] = s2[:, mine_y] + sy[0] + sy[1] + sy[2]
    small = []
    for d in range(1, 16):
        copy = remote(s3, sz.at[z], sz_s.at[d - 1], sz_r.at[d - 1], peer_z(d))
        copy.start()
        small.append(copy)
    sz[z] = s3[...]

    @pl.when(top)
    def _():
        fold_next(1, 2)

    for copy in along:
        copy.wait()
    parts = []
    for k in range(2):
        mine = h2[k, (y, x)[k]].astype(F32)
        mine = mine + r2[k, 0].astype(F32) + r2[k, 1].astype(F32) + r2[k, 2].astype(F32)
        parts.append(mine.astype(BF16))
    pick_up = onehot(128, 256, lambda p: jnp.where(p % 128 < 48, p // 128 * 48 + p % 128, -1))
    pick_down = onehot(
        96, 256, lambda p: jnp.where((p % 128 >= 64) & (p % 128 < 112), p // 128 * 48 + p % 128 - 64, -1)
    )
    both = dot(parts[0], pick_up) + dot(parts[1], pick_down, (0, 0))[0:96]
    rows_to = onehot(96, 128, lambda p: jnp.where(p % 16 < 12, p // 16 * 12 + p % 16, -1))
    tiles = dot(rows_to, both.astype(BF16), (0, 0)).astype(BF16)
    for q in range(16):
        t[q] = tiles[q % 8 * 16 : q % 8 * 16 + 16, q // 8 * 128 : q // 8 * 128 + 128]
    along = []
    for d in range(1, 16):
        copy = remote(t.at[lax.rem(z + d, 16)], tz.at[d - 1], z_s.at[d - 1], z_r.at[d - 1], peer_z(d))
        copy.start()
        along.append(copy)

    finish_rows(third)
    fourth = corners(dv, ew, ee, es, er)
    widen_rows(dwide, dv, 0)

    @pl.when(jnp.logical_not(top))
    def _():
        widen_rows(dwide, dv, 1)

    @pl.when(top)
    def _():
        dwide[:, ROWS + PAD :] = jnp.zeros((3, PAD, WIDE, 128), F32)
        fold_next(1, 3)

    for copy in small:
        copy.wait()
    total = sz[0]
    for q in range(1, 16):
        total = total + sz[q]
    b1[:, mine_y] = total * FACTOR
    gather = []
    for d in range(1, 4):
        copy = remote(b1.at[:, mine_y], b1.at[:, mine_y], gy_s.at[d - 1], gy_r.at[d - 1], peer_y(d))
        copy.start()
        gather.append(copy)

    finish_corners(dwide, fourth, ew, ee)
    conv_part(dwide, taps, True, beyond, ((0, COLS),), read_bacc, put_back)

    for copy in gather:
        copy.wait()
    b2[x] = b1[...]
    gather = []
    for d in range(1, 4):
        copy = remote(b1, b2.at[x], gx_s.at[d - 1], gx_r.at[d - 1], peer_x(d))
        copy.start()
        gather.append(copy)

    for copy in along:
        copy.wait()
    total = t[z].astype(F32)
    for d in range(15):
        total = total + tz[d].astype(F32)
    tile_out[...] = total * FACTOR

    for copy in gather:
        copy.wait()
    b3[c] = b2[...]
    copy = remote(b2, b3.at[c], gc_s.at[0], gc_r.at[0], other)
    copy.start()

    @pl.when(top)
    def _():
        ghost = fold_last(1)
        for ct in range(3):
            for q in range(PAD):
                edge[ct, q] = ghost[q * WIDE : (q + 1) * WIDE, ct * 128 : ct * 128 + 128]

        def read_edge(j, lanes):
            return edge_rows[j, :, lanes]

        def put_edge(j, lanes, value):
            gs_out[4 + j, :, lanes] = value.astype(BF16)

        fold_into(edge, taps, read_edge, put_edge)

    copy.wait()
    small_out[...] = b3[...].reshape(64, 512)


def finish(gs_in, tile_in, small_in, gs_out, up_out, down_out, gk_out, gc_out, gb_out):
    gs_out[...] = gs_in[...]
    up_out[...] = tile_in[0:12, 0:48]
    down_out[...] = tile_in[0:12, 64:112]
    gk_out[...] = small_in[0:49, 0:CH]
    gc_out[...] = small_in[49:53, 0:CH]
    gb_out[0:CH] = small_in[53, 0:CH]
    gb_out[CH:HID] = small_in[54, 0:CH]


def fused(*args):
    sds = jax.ShapeDtypeStruct
    vm = pltpu.VMEM
    dma = pltpu.SemaphoreType.DMA
    hbm_spec = pl.BlockSpec(memory_space=pltpu.HBM)
    vm_spec = pl.BlockSpec(memory_space=pltpu.VMEM)
    edge16 = (ROWS, 16, CH)
    corner = (2, PAD, 16, CH)
    scratch = [
        vm((ROWS, COLS, CH), BF16), vm((ROWS, COLS, CH), BF16), vm((ROWS, COLS), jnp.int32), vm((1, 1), jnp.int32),
        vm((49, CH), F32), vm((CH,), F32), vm((CH,), F32), vm((CH, HID), BF16), vm((HID,), F32),
        vm((CH, HID), BF16), vm((CH,), F32), vm((CH,), F32),
        vm(edge16, BF16), vm(edge16, BF16), vm((2, PAD, COLS, CH), BF16), vm(corner, BF16), vm(corner, BF16),
        vm(edge16, BF16), vm(edge16, BF16), vm((2, PAD, COLS, CH), BF16), vm(corner, BF16), vm(corner, BF16),
        vm((3, 14, WIDE, 128), F32), vm((3, 14, WIDE, 128), F32), vm((3, PAD, WIDE, 128), F32),
        vm((3, ROWS, COLS, 128), F32), vm((3, ROWS, COLS, 128), F32), vm((PAD, COLS, CH), F32),
        vm((CH, HID), BF16), vm((CH, HID), BF16), vm((1, HID), F32),
        vm((CELLS, CH), F32), vm((CELLS, 1), F32), vm((CELLS, CH), BF16),
        vm((CELLS, CH), F32), vm((CELLS, CH), BF16), vm((CELLS, HID), F32), vm((CELLS // 2, HID), F32),
        vm((CELLS, HID), BF16), vm((CELLS, HID), BF16), vm((CELLS // 2, CH), F32),
        vm((3, ROWS, COLS, 128), F32), vm((ROWS, COLS, CH), BF16),
        vm((2, 2, 384, 384), BF16), vm((2, 384, 384), BF16), vm((2, 4, 96, 384), BF16),
        vm((2, 3, 96, 384), BF16), vm((2, 4, 96, 128), BF16), vm((2, 3, 96, 128), BF16),
        vm((16, 16, 128), BF16), vm((15, 16, 128), BF16), vm((HID, HID), BF16),
        vm((64, 512), F32), vm((32, 512), F32), vm((4, 8, 512), F32), vm((3, 8, 512), F32), vm((8, 512), F32),
        vm((3, 8, 128), F32), vm((8, 128), F32), vm((16, 8, 128), F32), vm((8, 512), F32), vm((4, 8, 512), F32),
        vm((2, 4, 8, 512), F32), vm((2, 4, 2, 8, 16, CH), BF16),
        dma((12,)), dma((4,)), dma((4,)), dma((4,)), dma((4,)), dma((4,)), dma((4,)), dma((4,)), dma((4,)),
        dma((1,)), dma((1,)), dma((2, 3)), dma((2, 3)), dma((2, 3)), dma((2, 3)), dma((15,)), dma((15,)),
        dma((1,)), dma((1,)), dma((3,)), dma((3,)), dma((3,)), dma((3,)), dma((15,)), dma((15,)),
        dma((3,)), dma((3,)), dma((3,)), dma((3,)), dma((1,)), dma((1,)), dma((2, 4, 7)), dma((2, 4, 7)),
    ]
    return pl.pallas_call(
        body,
        out_shape=[sds((ROWS, COLS, CH), BF16), sds((16, 128), F32), sds((64, 512), F32)],
        in_specs=[hbm_spec] * 12,
        out_specs=[vm_spec] * 3,
        scratch_shapes=scratch,
        compiler_params=pltpu.CompilerParams(
            collective_id=0, has_side_effects=True, vmem_limit_bytes=63 * 2**20
        ),
        name="block",
    )(*args)


def local(
    state, cotangent, ocean, fold_partner, kernel, ln_gain, ln_shift, w_up, b_up, w_down, b_down, layer_scale
):
    results = fused(
        state, cotangent, ocean, fold_partner[None], kernel, ln_gain, ln_shift, w_up, b_up,
        w_down, b_down, layer_scale,
    )
    sds = jax.ShapeDtypeStruct
    grad_state, up, down, g_kernel, g_chan, g_bup = (
        pl.pallas_call(
            finish,
            out_shape=[
                sds((ROWS, COLS, CH), BF16), sds((12, 48), F32), sds((12, 48), F32),
                sds((49, CH), F32), sds((4, CH), F32), sds((HID,), F32),
            ],
            name="outputs",
        )(*results)
    )
    return grad_state, up.T, down.T, g_kernel, g_chan, g_bup


def solution(mesh):
    placed = (P("ja", "ia", None), P("ja", "ia", None), P("ja", "ia"), P("ia")) + (P(),) * 8
    return jax.shard_map(
        local,
        mesh=mesh,
        in_specs=placed,
        out_specs=(P("ja", "ia", None), P("ja", "ia"), P("ja", "ia"), P(), P(), P()),
        check_vma=False,
    )
```

```python
import functools
import math

import jax
import jax.numpy as jnp
from jax import lax
from jax.experimental import pallas as pl
from jax.experimental.pallas import tpu as pltpu
from jax.sharding import PartitionSpec as P

KW = 7
PAD = 3
ROWS = 8
COLS = 32
CH = 384
HID = 768
CELLS = ROWS * COLS
WIDE = 48
F32 = jnp.float32
BF16 = jnp.bfloat16
LANES = 64
BANDS = 8
COEFF = 0.7978845608028654
CUBIC = 0.044715
FACTOR = 1.0 / math.sqrt(ROWS * BANDS * COLS * LANES)


def place(x, y, z, c):
    return {"ia": x * 16 + lax.rem(z, 8) * 2 + c, "ja": y * 2 + z // 8}


def dot(a, b, dims=(1, 0)):
    return lax.dot_general(
        a, b, (((dims[0],), (dims[1],)), ((), ())), preferred_element_type=F32
    )


def sub8(v):
    return v[0:8] + v[8:16] + v[16:24] + v[24:32]


def onehot(rows, cols, target):
    want = target(lax.broadcasted_iota(jnp.int32, (1, cols), 1))
    here = lax.broadcasted_iota(jnp.int32, (rows, cols), 0)
    return jnp.where(here == want, 1.0, 0.0).astype(BF16)


def split3(v):
    hi = v.astype(BF16)
    rest = v - hi.astype(F32)
    mid = rest.astype(BF16)
    low = (rest - mid.astype(F32)).astype(BF16)
    zeros = jnp.zeros((13, v.shape[1]), F32)
    return jnp.concatenate(
        [hi.astype(F32), mid.astype(F32), low.astype(F32), zeros], axis=0
    ).astype(BF16)


def conv_part(wide, taps, flip, rows, outs, read, write):
    def tile(ct, _):
        lanes = pl.ds(pl.multiple_of(ct * 128, 128), 128)
        hit = [j for j in outs if any(0 <= r - j < KW for r in rows)]
        total = {j: read(ct, j) for j in hit}
        for b in range(KW):
            weight = []
            for a in range(KW):
                tap = a * KW + b
                tap = KW * KW - 1 - tap if flip else tap
                weight.append(taps[tap : tap + 1, lanes])
            for r in rows:
                value = wide[ct, r, 5 + b : 5 + b + COLS, :]
                for a in range(KW):
                    if r - a in total:
                        total[r - a] = total[r - a] + value * weight[a]
        for j in hit:
            write(ct, lanes, j, total[j])
        return 0

    lax.fori_loop(0, 3, tile, 0)


def fold_into(edge, taps, read, write):
    def tile(ct, _):
        lanes = pl.ds(pl.multiple_of(ct * 128, 128), 128)
        total = [read(j, lanes) for j in range(3)]
        for b in range(KW):
            for j in range(3):
                for e in range(j + 1):
                    a = e + 6 - j
                    weight = taps[a * KW + b : a * KW + b + 1, lanes]
                    total[j] = total[j] + edge[ct, e, 5 + b : 5 + b + COLS, :] * weight
        for j in range(3):
            write(j, lanes, total[j])
        return 0

    lax.fori_loop(0, 3, tile, 0)


def fold_slots(p):
    q = jnp.where(p < 112, p - 96, p - 112)
    first = q // 3 * COLS + q % 3
    edge = jnp.where(q < 9, jnp.where(p < 112, first, first + COLS - 3), -1)
    return jnp.where(p < 96, p, edge)


def fold_cells(p):
    row, col = p // WIDE, p % WIDE
    west = 96 + (2 - row) * 3 + 7 - col
    east = 112 + (2 - row) * 3 + 42 - col
    inner = 95 - row * COLS - (col - 8)
    slot = jnp.where(col < 8, west, jnp.where(col < 40, inner, east))
    return jnp.where((col >= 5) & (col < 43), slot, -1)


def fold_swap(p):
    return p % 16 // 2 * 16 + p // 16 * 2 + p % 2


def body(
    state, cot, ocean, partner, taps_in, gain_in, shift_in, wup_in, bup_in, wdown_in, bdown_in, scale_in,
    gs_out, tile_out, small_out,
    xs, cs, oc, part, taps, gain, shift, wup0, bup0, wdown0, bdown, scale,
    hw, he, hv, cw, ce, dw, de, dv, ew, ee,
    wide, dwide, edge, acc, bacc, edge_rows, wup, wdown, bup,
    unit, rstd, normed, masked, dbr, dhid, pre, hidden, dpre, dnorm, dcv, dcb,
    g, gc, h, h1, h2, r2, t, tz, perm,
    s, sc, s1, sx, s2, sy, s3, sz, b1, b2, b3, fold,
    loc, hs, hr, qs, qr, ds, dr, es, er, cs_s, cs_r, f_s, f_r, k_s, k_r, z_s, z_r,
    sa_s, sa_r, sx_s, sx_r, sy_s, sy_r, sz_s, sz_r, gy_s, gy_r, gx_s, gx_r, gc_s, gc_r, fold_s, fold_r,
):
    ia, ja = lax.axis_index("ia"), lax.axis_index("ja")
    x, zl, c = ia // 16, lax.rem(ia // 2, 8), lax.rem(ia, 2)
    y, zh = ja // 2, lax.rem(ja, 2)
    z = zh * 8 + zl
    u = x * 2 + c
    top, bottom = ja == BANDS - 1, ja == 0
    east = {"ia": lax.rem(ia + 1, LANES), "ja": ja}
    west = {"ia": lax.rem(ia + LANES - 1, LANES), "ja": ja}
    north = {"ia": ia, "ja": ja + 1}
    south = {"ia": ia, "ja": ja - 1}

    def remote(src, dst, send, recv, device):
        return pltpu.make_async_remote_copy(
            src_ref=src, dst_ref=dst, send_sem=send, recv_sem=recv,
            device_id=device, device_id_type=pl.DeviceIdType.MESH,
        )

    def peer_x(d):
        return place(lax.rem(x + d, 4), y, z, c)

    def peer_y(d):
        return place(x, lax.rem(y + d, 4), z, c)

    def peer_z(d):
        return place(x, y, lax.rem(z + d, 16), c)

    def peer_u(d):
        to = lax.rem(u + d, 8)
        return {"ia": to // 2 * 16 + zl * 2 + lax.rem(to, 2), "ja": ja}

    def peer_v(d):
        return {"ia": x * 16 + lax.rem(zl + d, 8) * 2 + c, "ja": ja}

    other = place(x, y, z, 1 - c)

    loads = [
        pltpu.make_async_copy(src, dst, loc.at[i])
        for i, (src, dst) in enumerate(
            [
                (state, xs), (cot, cs), (ocean, oc), (taps_in, taps), (gain_in, gain), (shift_in, shift),
                (wup_in, wup0), (bup_in, bup0), (wdown_in, wdown0), (bdown_in, bdown), (scale_in, scale),
                (partner, part),
            ]
        )
    ]
    for load in loads:
        load.start()

    barrier = pltpu.get_barrier_semaphore()

    def greet(device):
        pl.semaphore_signal(barrier, inc=1, device_id=device, device_id_type=pl.DeviceIdType.MESH)

    greet({"ia": ia, "ja": lax.rem(ja + 1, BANDS)})
    greet({"ia": ia, "ja": lax.rem(ja + BANDS - 1, BANDS)})
    greet(east)
    greet(west)

    @pl.when(top)
    def _():
        for d in range(1, 8):
            greet(peer_u(d))
            greet(peer_v(d))

    for d in range(1, 16):
        greet(peer_z(d))
    for d in range(1, 4):
        greet(peer_x(d))
        greet(peer_y(d))
    greet(other)

    for load in loads:
        load.wait()

    def old(p):
        return (p % 384) // 96 * 192 + (p % 96) // 12 * 24 + p // 384 * 12 + p % 12

    perm[...] = onehot(HID, HID, old)
    wup[...] = dot(wup0[...], perm[...]).astype(BF16)
    wdown[...] = dot(wdown0[...], perm[...]).astype(BF16)
    bup[...] = jnp.sum(dot(split3(bup0[...][None]), perm[...]), axis=0, keepdims=True)

    eye = (
        lax.broadcasted_iota(jnp.int32, (COLS, COLS), 0)
        == lax.broadcasted_iota(jnp.int32, (COLS, COLS), 1)
    ).astype(F32)

    def mask_row(j, total):
        sea = jnp.sum(eye * oc[pl.ds(j, 1), :].astype(F32), axis=1, keepdims=True)
        cells = pl.ds(pl.multiple_of(j * COLS, COLS), COLS)
        value = cs[j].astype(F32) * sea
        masked[cells, :] = value
        dbr[cells, :] = (value * scale[...][None]).astype(BF16)
        return total + sub8(value * scale[...][None])

    g_bdown = lax.fori_loop(0, ROWS, mask_row, jnp.zeros((8, CH), F32))
    dhid[...] = dot(dbr[...], wdown[...])

    def widen_own(dst, centre):
        for ct in range(3):
            lanes = slice(ct * 128, ct * 128 + 128)
            for r in range(ROWS):
                dst[ct, PAD + r, 8:40, :] = centre[r, :, lanes].astype(F32)

    def widen_sides(dst, w, e):
        for ct in range(3):
            lanes = slice(ct * 128, ct * 128 + 128)
            for r in range(ROWS):
                dst[ct, PAD + r, 0:8, :] = w[r, :, lanes].astype(F32)[8:16]
                dst[ct, PAD + r, 40:48, :] = e[r, :, lanes].astype(F32)[0:8]

    def widen_rows(dst, v, k):
        for ct in range(3):
            lanes = slice(ct * 128, ct * 128 + 128)
            for q in range(PAD):
                dst[ct, q + k * (ROWS + PAD), 8:40, :] = v[k, q, :, lanes].astype(F32)

    def widen_corners(dst, w, e, k):
        for ct in range(3):
            lanes = slice(ct * 128, ct * 128 + 128)
            for q in range(PAD):
                dst[ct, q + k * (ROWS + PAD), 0:8, :] = w[k, q, :, lanes].astype(F32)[8:16]
                dst[ct, q + k * (ROWS + PAD), 40:48, :] = e[k, q, :, lanes].astype(F32)[0:8]

    widen_own(wide, xs)

    pl.semaphore_wait(barrier, 26 + jnp.where(top, 14, 0))

    def halo(src, w, e, v, send, recv):
        return (
            remote(src.at[5:8], v.at[0], send.at[0], recv.at[0], north),
            remote(src.at[0:3], v.at[1], send.at[1], recv.at[1], south),
            remote(src.at[:, 16:32], w, send.at[2], recv.at[2], east),
            remote(src.at[:, 0:16], e, send.at[3], recv.at[3], west),
        )

    def start_south(copies):
        @pl.when(jnp.logical_not(bottom))
        def _():
            copies[1].start()

    def start_rest(copies):
        @pl.when(jnp.logical_not(top))
        def _():
            copies[0].start()

        copies[2].start()
        copies[3].start()

    def finish_south(copies):
        @pl.when(jnp.logical_not(bottom))
        def _():
            copies[1].wait_send()
            copies[0].wait_recv()

    def finish_north(copies):
        @pl.when(jnp.logical_not(top))
        def _():
            copies[0].wait_send()
            copies[1].wait_recv()

    def corners(v, w, e, send, recv):
        copies = []
        for k in range(2):
            copies.append(remote(v.at[k, :, 16:32], w.at[k], send.at[2 * k], recv.at[2 * k], east))
            copies.append(remote(v.at[k, :, 0:16], e.at[k], send.at[2 * k + 1], recv.at[2 * k + 1], west))
        return copies

    def rows_arrived(dst, copies, v, w, e, send, recv):
        passed = corners(v, w, e, send, recv)
        finish_south(copies)
        passed[0].start()
        passed[1].start()
        widen_rows(dst, v, 0)
        finish_north(copies)

        @pl.when(jnp.logical_not(top))
        def _():
            passed[2].start()
            passed[3].start()
            widen_rows(dst, v, 1)

        return passed

    def finish_corners_south(dst, copies, w, e):
        copies[0].wait()
        copies[1].wait()
        widen_corners(dst, w, e, 0)

    def finish_corners_north(dst, copies, w, e):
        @pl.when(jnp.logical_not(top))
        def _():
            copies[2].wait()
            copies[3].wait()
            widen_corners(dst, w, e, 1)

    def fold_copies(k, step, peer, me):
        return [
            remote(
                fold.at[k, step, 0, lax.rem(me + d, 8)], fold.at[k, step, 1, me],
                fold_s.at[k, step, d - 1], fold_r.at[k, step, d - 1], peer(d),
            )
            for d in range(1, 8)
        ]

    fold_steps = ((peer_u, u), (peer_v, zl), (peer_v, zl), (peer_u, u))

    def fold_send(k, step, value):
        peer, me = fold_steps[step]
        fold[k, step, 0] = value.astype(BF16).reshape(8, 16, CH)
        for copy in fold_copies(k, step, peer, me):
            copy.start()
        fold[k, step, 1, me] = fold[k, step, 0, me]

    def fold_take(k, step):
        peer, me = fold_steps[step]
        for copy in fold_copies(k, step, peer, me):
            copy.wait()
        return fold[k, step, 1].reshape(128, CH)

    def fold_first(k, strip):
        fold_send(k, 0, dot(onehot(96, 128, fold_slots), strip, (0, 0)))

    def fold_next(k, step):
        value = fold_take(k, step - 1)

        def facing(p):
            into = p % 16 // 2
            target = into // 2 * 16 + p // 16 * 2 + into % 2
            shift = jnp.where(u == 6, 1, 0) - jnp.where(u == 7, 1, 0)
            source = (part[...] + ia - target + shift + LANES) % LANES
            return source // 2 % 8 * 16 + (source // 16 * 2 + source % 2) * 2 + p % 2

        matrix = onehot(128, 128, facing if step == 2 else fold_swap)
        fold_send(k, step, dot(matrix, value, (0, 0)))

    def fold_last(k):
        return dot(onehot(128, PAD * WIDE, fold_cells), fold_take(k, 3), (0, 0))

    first = halo(state, hw, he, hv, hs, hr)
    start_south(first)
    start_rest(first)

    @pl.when(top)
    def _():
        fold_first(0, xs[4:7].reshape(96, CH))

    @pl.when(bottom)
    def _():
        hv[0] = jnp.zeros((PAD, COLS, CH), BF16)

    own, south_rows, north_rows = tuple(range(PAD, PAD + ROWS)), (0, 1, 2), (11, 12, 13)
    every = tuple(range(ROWS))

    def nothing(ct, j):
        return jnp.zeros((COLS, 128), F32)

    def read_acc(ct, j):
        return acc[ct, j]

    def write_acc(ct, lanes, j, value):
        acc[ct, j] = value

    for copy in first[2:]:
        copy.wait()
    widen_sides(wide, hw, he)

    @pl.when(top)
    def _():
        fold_next(0, 1)

    conv_part(wide, taps, False, own, every, nothing, write_acc)

    @pl.when(top)
    def _():
        fold_next(0, 2)

    second = rows_arrived(wide, first, hv, cw, ce, qs, qr)

    @pl.when(top)
    def _():
        fold_next(0, 3)

    def half_pass(k):
        base = k * 128
        block = slice(base, base + 128)
        beyond = (south_rows, north_rows)[k]
        conv_part(wide, taps, False, beyond, every[4 * k : 4 * k + 4], read_acc, write_acc)

        def norm_rows(i, _):
            cells = pl.ds(pl.multiple_of(base + i * 32, 32), 32)
            value = jnp.concatenate([acc[ct, 4 * k + i] for ct in range(3)], axis=1)
            value = value - jnp.mean(value, axis=1, keepdims=True)
            r = lax.rsqrt(jnp.mean(value * value, axis=1, keepdims=True) + 1e-06)
            value = value * r
            rstd[cells, :] = r
            unit[cells, :] = value
            normed[cells, :] = (value * gain[...][None] + shift[...][None]).astype(BF16)
            return 0

        lax.fori_loop(0, 4, norm_rows, 0)
        pre[...] = dot(normed[block, :], wup[...])

        def gelu_rows(i, totals):
            here = pl.ds(pl.multiple_of(i * 32, 32), 32)
            cells = pl.ds(pl.multiple_of(base + i * 32, 32), 32)
            done = []
            for q in range(3):
                lanes = slice(q * 256, q * 256 + 256)
                v = pre[here, lanes] + bup[:, lanes]
                square = v * v
                tanh = jnp.tanh(v * (COEFF + COEFF * CUBIC * square))
                half = 0.5 + 0.5 * tanh
                value = v * half
                slope = half + value * (1.0 - tanh) * (COEFF + 3.0 * CUBIC * COEFF * square)
                hidden[cells, lanes] = value.astype(BF16)
                grad = dhid[cells, lanes] * slope
                dpre[cells, lanes] = grad.astype(BF16)
                done.append(totals[q] + sub8(grad))
            return tuple(done)

        bias = lax.fori_loop(0, 4, gelu_rows, tuple(jnp.zeros((8, 256), F32) for _ in range(3)))
        dnorm[...] = dot(dpre[block, :], wup[...], (1, 1))

        def back_rows(i, totals):
            here = pl.ds(pl.multiple_of(i * 32, 32), 32)
            cells = pl.ds(pl.multiple_of(base + i * 32, 32), 32)
            unit_rows = unit[cells, :]
            grad = dnorm[here, :]
            product = grad * unit_rows
            scaled = grad * gain[...][None]
            mean_a = jnp.mean(scaled, axis=1, keepdims=True)
            mean_b = jnp.mean(product * gain[...][None], axis=1, keepdims=True)
            value = rstd[cells, :] * (scaled - mean_a - unit_rows * mean_b)
            value = value.astype(BF16)
            dcb[4 * k + i] = value
            value = value.astype(F32)
            for ct in range(3):
                dcv[ct, 4 * k + i] = value[:, ct * 128 : ct * 128 + 128]
            return totals[0] + sub8(product), totals[1] + sub8(grad)

        zero = jnp.zeros((8, CH), F32)
        return bias, lax.fori_loop(0, 4, back_rows, (zero, zero))

    @pl.when(bottom)
    def _():
        dv[0] = jnp.zeros((PAD, COLS, CH), BF16)

    finish_corners_south(wide, second, cw, ce)
    bias_a, norm_a = half_pass(0)
    third = halo(dcb, dw, de, dv, ds, dr)
    start_south(third)

    finish_corners_north(wide, second, cw, ce)

    @pl.when(top)
    def _():
        ghost = fold_last(0)
        for ct in range(3):
            for q in range(PAD):
                wide[ct, ROWS + PAD + q] = ghost[q * WIDE : (q + 1) * WIDE, ct * 128 : ct * 128 + 128]

    bias_b, norm_b = half_pass(1)

    start_rest(third)

    @pl.when(top)
    def _():
        fold_first(1, dcb[5:8].reshape(96, CH))

    def tap_tile(ct, _):
        lanes = pl.ds(pl.multiple_of(ct * 128, 128), 128)
        for b in range(KW):
            total = [jnp.zeros((8, 128), F32) for _ in range(KW)]
            for r in range(ROWS + 2 * PAD):
                value = wide[ct, r, 5 + b : 5 + b + COLS, :]
                for a in range(KW):
                    j = r - a
                    if 0 <= j < ROWS:
                        total[a] = total[a] + sub8(value * dcv[ct, j])
            for a in range(KW):
                s[a * KW + b : a * KW + b + 1, lanes] = jnp.sum(total[a], axis=0, keepdims=True)
        return 0

    s[...] = jnp.zeros((64, 512), F32)
    lax.fori_loop(0, 3, tap_tile, 0)

    branch = dot(hidden[...], wdown[...], (1, 1)) + bdown[...][None]
    g_scale = jnp.sum(masked[...] * branch, axis=0, keepdims=True)
    g_bup = jnp.concatenate(
        [jnp.sum(va + vb, axis=0, keepdims=True) for va, vb in zip(bias_a, bias_b)], axis=1
    )
    back = jnp.sum(dot(split3(g_bup), perm[...], (1, 1)), axis=0, keepdims=True)
    s[49:50, 0:CH] = jnp.sum(norm_a[0] + norm_b[0], axis=0, keepdims=True)
    s[50:51, 0:CH] = jnp.sum(norm_a[1] + norm_b[1], axis=0, keepdims=True)
    s[51:52, 0:CH] = jnp.sum(g_bdown, axis=0, keepdims=True)
    s[52:53, 0:CH] = g_scale
    s[53:54, 0:CH] = back[:, 0:CH]
    s[54:55, 0:CH] = back[:, CH:HID]
    half_s = pl.multiple_of((1 - c) * 32, 32)
    cross_s = remote(s.at[pl.ds(half_s, 32)], sc, sa_s.at[0], sa_r.at[0], other)
    cross_s.start()

    for half in range(2):
        units = slice(half * 384, half * 384 + 384)
        g[0, half] = dot(dpre[:, units], normed[...], (0, 0)).astype(BF16)
        g[1, half] = dot(dbr[...], hidden[:, units], (0, 0)).astype(BF16)
    cross = remote(g.at[:, 1 - c], gc, cs_s.at[0], cs_r.at[0], other)
    cross.start()

    cross_s.wait()
    mine_s = pl.multiple_of(c * 32, 32)
    s1[...] = (s[pl.ds(mine_s, 32), :] + sc[...]).reshape(4, 8, 512)
    small = []
    for d in range(1, 4):
        copy = remote(s1.at[lax.rem(x + d, 4)], sx.at[d - 1], sx_s.at[d - 1], sx_r.at[d - 1], peer_x(d))
        copy.start()
        small.append(copy)

    cross.wait()
    for k in range(2):
        for q in range(4):
            rows = slice(q * 96, q * 96 + 96)
            h[k, q] = (g[k, c, rows, :].astype(F32) + gc[k, rows, :].astype(F32)).astype(BF16)
    along = []
    for d in range(1, 4):
        up = remote(h.at[0, lax.rem(x + d, 4)], h1.at[0, d - 1], f_s.at[0, d - 1], f_r.at[0, d - 1], peer_x(d))
        down = remote(h.at[1, lax.rem(y + d, 4)], h1.at[1, d - 1], f_s.at[1, d - 1], f_r.at[1, d - 1], peer_y(d))
        up.start()
        down.start()
        along += [up, down]

    def put_back(ct, lanes, j, value):
        value = cs[j, :, lanes].astype(F32) + value
        gs_out[j, :, lanes] = value.astype(BF16)
        if 4 <= j < 7:
            edge_rows[j - 4, :, lanes] = value

    def write_bacc(ct, lanes, j, value):
        if 3 <= j < 5:
            put_back(ct, lanes, j, value)
        else:
            bacc[ct, j] = value

    def read_bacc(ct, j):
        return bacc[ct, j]

    widen_own(dwide, dcb)

    for copy in small:
        copy.wait()
    s2[...] = s1[x] + sx[0] + sx[1] + sx[2]
    small = []
    for d in range(1, 4):
        chunk = pl.ds(pl.multiple_of(lax.rem(y + d, 4) * 128, 128), 128)
        copy = remote(s2.at[:, chunk], sy.at[d - 1], sy_s.at[d - 1], sy_r.at[d - 1], peer_y(d))
        copy.start()
        small.append(copy)

    for copy in third[2:]:
        copy.wait()
    widen_sides(dwide, dw, de)
    conv_part(dwide, taps, True, own, every, nothing, write_bacc)

    for copy in small:
        copy.wait()
    mine_y = pl.ds(pl.multiple_of(y * 128, 128), 128)
    s3[...] = s2[:, mine_y] + sy[0] + sy[1] + sy[2]
    small = []
    for d in range(1, 16):
        copy = remote(s3, sz.at[z], sz_s.at[d - 1], sz_r.at[d - 1], peer_z(d))
        copy.start()
        small.append(copy)
    sz[z] = s3[...]

    for copy in along:
        copy.wait()
    spread = onehot(CH, 512, lambda p: jnp.where(p % 128 < 96, p // 128 * 96 + p % 128, -1))
    for k in range(2):
        mine = h[k, (x, y)[k]].astype(F32)
        mine = mine + h1[k, 0].astype(F32) + h1[k, 1].astype(F32) + h1[k, 2].astype(F32)
        mine = dot(mine.astype(BF16), spread).astype(BF16)
        for q in range(4):
            h2[k, q] = mine[:, q * 128 : q * 128 + 128]
    along = []
    for d in range(1, 4):
        up = remote(h2.at[0, lax.rem(y + d, 4)], r2.at[0, d - 1], k_s.at[0, d - 1], k_r.at[0, d - 1], peer_y(d))
        down = remote(h2.at[1, lax.rem(x + d, 4)], r2.at[1, d - 1], k_s.at[1, d - 1], k_r.at[1, d - 1], peer_x(d))
        up.start()
        down.start()
        along += [up, down]

    @pl.when(top)
    def _():
        fold_next(1, 1)

    for copy in along:
        copy.wait()
    parts = []
    for k in range(2):
        mine = h2[k, (y, x)[k]].astype(F32)
        mine = mine + r2[k, 0].astype(F32) + r2[k, 1].astype(F32) + r2[k, 2].astype(F32)
        parts.append(mine.astype(BF16))
    pick_up = onehot(128, 256, lambda p: jnp.where(p % 128 < 48, p // 128 * 48 + p % 128, -1))
    pick_down = onehot(
        96, 256, lambda p: jnp.where((p % 128 >= 64) & (p % 128 < 112), p // 128 * 48 + p % 128 - 64, -1)
    )
    both = dot(parts[0], pick_up) + dot(parts[1], pick_down, (0, 0))[0:96]
    rows_to = onehot(96, 128, lambda p: jnp.where(p % 16 < 12, p // 16 * 12 + p % 16, -1))
    tiles = dot(rows_to, both.astype(BF16), (0, 0)).astype(BF16)
    for q in range(16):
        t[q] = tiles[q % 8 * 16 : q % 8 * 16 + 16, q // 8 * 128 : q // 8 * 128 + 128]
    along = []
    for d in range(1, 16):
        copy = remote(t.at[lax.rem(z + d, 16)], tz.at[d - 1], z_s.at[d - 1], z_r.at[d - 1], peer_z(d))
        copy.start()
        along.append(copy)

    fourth = rows_arrived(dwide, third, dv, ew, ee, es, er)

    @pl.when(top)
    def _():
        dwide[:, ROWS + PAD :] = jnp.zeros((3, PAD, WIDE, 128), F32)

    @pl.when(top)
    def _():
        fold_next(1, 2)

    for copy in small:
        copy.wait()
    total = sz[0]
    for q in range(1, 16):
        total = total + sz[q]
    b1[:, mine_y] = total * FACTOR
    gather = []
    for d in range(1, 4):
        copy = remote(b1.at[:, mine_y], b1.at[:, mine_y], gy_s.at[d - 1], gy_r.at[d - 1], peer_y(d))
        copy.start()
        gather.append(copy)

    for copy in gather:
        copy.wait()
    b2[x] = b1[...]
    gather = []
    for d in range(1, 4):
        copy = remote(b1, b2.at[x], gx_s.at[d - 1], gx_r.at[d - 1], peer_x(d))
        copy.start()
        gather.append(copy)

    @pl.when(top)
    def _():
        fold_next(1, 3)

    finish_corners_south(dwide, fourth, ew, ee)
    finish_corners_north(dwide, fourth, ew, ee)
    conv_part(dwide, taps, True, south_rows + north_rows, every, read_bacc, put_back)

    for copy in gather:
        copy.wait()
    b3[c] = b2[...]
    last = remote(b2, b3.at[c], gc_s.at[0], gc_r.at[0], other)
    last.start()

    for copy in along:
        copy.wait()
    total = t[z].astype(F32)
    for d in range(15):
        total = total + tz[d].astype(F32)
    tile_out[...] = total * FACTOR

    @pl.when(top)
    def _():
        ghost = fold_last(1)
        for ct in range(3):
            for q in range(PAD):
                edge[ct, q] = ghost[q * WIDE : (q + 1) * WIDE, ct * 128 : ct * 128 + 128]

        def read_edge(j, lanes):
            return edge_rows[j, :, lanes]

        def put_edge(j, lanes, value):
            gs_out[4 + j, :, lanes] = value.astype(BF16)

        fold_into(edge, taps, read_edge, put_edge)

    last.wait()
    small_out[...] = b3[...].reshape(64, 512)


def finish(gs_in, tile_in, small_in, gs_out, up_out, down_out, gk_out, gc_out, gb_out):
    gs_out[...] = gs_in[...]
    up_out[...] = tile_in[0:12, 0:48]
    down_out[...] = tile_in[0:12, 64:112]
    gk_out[...] = small_in[0:49, 0:CH]
    gc_out[...] = small_in[49:53, 0:CH]
    gb_out[0:CH] = small_in[53, 0:CH]
    gb_out[CH:HID] = small_in[54, 0:CH]


def fused(*args):
    sds = jax.ShapeDtypeStruct
    vm = pltpu.VMEM
    dma = pltpu.SemaphoreType.DMA
    hbm_spec = pl.BlockSpec(memory_space=pltpu.HBM)
    vm_spec = pl.BlockSpec(memory_space=pltpu.VMEM)
    edge16 = (ROWS, 16, CH)
    corner = (2, PAD, 16, CH)
    scratch = [
        vm((ROWS, COLS, CH), BF16), vm((ROWS, COLS, CH), BF16), vm((ROWS, COLS), jnp.int32), vm((1, 1), jnp.int32),
        vm((49, CH), F32), vm((CH,), F32), vm((CH,), F32), vm((CH, HID), BF16), vm((HID,), F32),
        vm((CH, HID), BF16), vm((CH,), F32), vm((CH,), F32),
        vm(edge16, BF16), vm(edge16, BF16), vm((2, PAD, COLS, CH), BF16), vm(corner, BF16), vm(corner, BF16),
        vm(edge16, BF16), vm(edge16, BF16), vm((2, PAD, COLS, CH), BF16), vm(corner, BF16), vm(corner, BF16),
        vm((3, 14, WIDE, 128), F32), vm((3, 14, WIDE, 128), F32), vm((3, PAD, WIDE, 128), F32),
        vm((3, ROWS, COLS, 128), F32), vm((3, ROWS, COLS, 128), F32), vm((PAD, COLS, CH), F32),
        vm((CH, HID), BF16), vm((CH, HID), BF16), vm((1, HID), F32),
        vm((CELLS, CH), F32), vm((CELLS, 1), F32), vm((CELLS, CH), BF16),
        vm((CELLS, CH), F32), vm((CELLS, CH), BF16), vm((CELLS, HID), F32), vm((CELLS // 2, HID), F32),
        vm((CELLS, HID), BF16), vm((CELLS, HID), BF16), vm((CELLS // 2, CH), F32),
        vm((3, ROWS, COLS, 128), F32), vm((ROWS, COLS, CH), BF16),
        vm((2, 2, 384, 384), BF16), vm((2, 384, 384), BF16), vm((2, 4, 96, 384), BF16),
        vm((2, 3, 96, 384), BF16), vm((2, 4, 96, 128), BF16), vm((2, 3, 96, 128), BF16),
        vm((16, 16, 128), BF16), vm((15, 16, 128), BF16), vm((HID, HID), BF16),
        vm((64, 512), F32), vm((32, 512), F32), vm((4, 8, 512), F32), vm((3, 8, 512), F32), vm((8, 512), F32),
        vm((3, 8, 128), F32), vm((8, 128), F32), vm((16, 8, 128), F32), vm((8, 512), F32), vm((4, 8, 512), F32),
        vm((2, 4, 8, 512), F32), vm((2, 4, 2, 8, 16, CH), BF16),
        dma((12,)), dma((4,)), dma((4,)), dma((4,)), dma((4,)), dma((4,)), dma((4,)), dma((4,)), dma((4,)),
        dma((1,)), dma((1,)), dma((2, 3)), dma((2, 3)), dma((2, 3)), dma((2, 3)), dma((15,)), dma((15,)),
        dma((1,)), dma((1,)), dma((3,)), dma((3,)), dma((3,)), dma((3,)), dma((15,)), dma((15,)),
        dma((3,)), dma((3,)), dma((3,)), dma((3,)), dma((1,)), dma((1,)), dma((2, 4, 7)), dma((2, 4, 7)),
    ]
    return pl.pallas_call(
        body,
        out_shape=[sds((ROWS, COLS, CH), BF16), sds((16, 128), F32), sds((64, 512), F32)],
        in_specs=[hbm_spec] * 12,
        out_specs=[vm_spec] * 3,
        scratch_shapes=scratch,
        compiler_params=pltpu.CompilerParams(
            collective_id=0, has_side_effects=True, vmem_limit_bytes=63 * 2**20
        ),
        name="block",
    )(*args)


def local(
    state, cotangent, ocean, fold_partner, kernel, ln_gain, ln_shift, w_up, b_up, w_down, b_down, layer_scale
):
    results = fused(
        state, cotangent, ocean, fold_partner[None], kernel, ln_gain, ln_shift, w_up, b_up,
        w_down, b_down, layer_scale,
    )
    sds = jax.ShapeDtypeStruct
    grad_state, up, down, g_kernel, g_chan, g_bup = (
        pl.pallas_call(
            finish,
            out_shape=[
                sds((ROWS, COLS, CH), BF16), sds((12, 48), F32), sds((12, 48), F32),
                sds((49, CH), F32), sds((4, CH), F32), sds((HID,), F32),
            ],
            name="outputs",
        )(*results)
    )
    return grad_state, up.T, down.T, g_kernel, g_chan, g_bup


def solution(mesh):
    placed = (P("ja", "ia", None), P("ja", "ia", None), P("ja", "ia"), P("ia")) + (P(),) * 8
    return jax.shard_map(
        local,
        mesh=mesh,
        in_specs=placed,
        out_specs=(P("ja", "ia", None), P("ja", "ia"), P("ja", "ia"), P(), P(), P()),
        check_vma=False,
    )
```

```python
import functools
import math

import jax
import jax.numpy as jnp
from jax import lax
from jax.experimental import pallas as pl
from jax.experimental.pallas import tpu as pltpu
from jax.sharding import PartitionSpec as P

KW = 7
PAD = 3
ROWS = 8
COLS = 32
CH = 384
HID = 768
CELLS = ROWS * COLS
WIDE = 48
F32 = jnp.float32
BF16 = jnp.bfloat16
LANES = 64
BANDS = 8
COEFF = 0.7978845608028654
CUBIC = 0.044715
FACTOR = 1.0 / math.sqrt(ROWS * BANDS * COLS * LANES)


def place(x, y, z, c):
    return {"ia": x * 16 + lax.rem(z, 8) * 2 + c, "ja": y * 2 + z // 8}


def dot(a, b, dims=(1, 0)):
    return lax.dot_general(
        a, b, (((dims[0],), (dims[1],)), ((), ())), preferred_element_type=F32
    )


def sub8(v):
    return v[0:8] + v[8:16] + v[16:24] + v[24:32]


def onehot(rows, cols, target):
    want = target(lax.broadcasted_iota(jnp.int32, (1, cols), 1))
    here = lax.broadcasted_iota(jnp.int32, (rows, cols), 0)
    return jnp.where(here == want, 1.0, 0.0).astype(BF16)


def split3(v):
    hi = v.astype(BF16)
    rest = v - hi.astype(F32)
    mid = rest.astype(BF16)
    low = (rest - mid.astype(F32)).astype(BF16)
    zeros = jnp.zeros((13, v.shape[1]), F32)
    return jnp.concatenate(
        [hi.astype(F32), mid.astype(F32), low.astype(F32), zeros], axis=0
    ).astype(BF16)


def conv_part(wide, taps, flip, rows, outs, read, write):
    def tile(ct, _):
        lanes = pl.ds(pl.multiple_of(ct * 128, 128), 128)
        hit = [j for j in outs if any(0 <= r - j < KW for r in rows)]
        total = {j: read(ct, j) for j in hit}
        for b in range(KW):
            weight = []
            for a in range(KW):
                tap = a * KW + b
                tap = KW * KW - 1 - tap if flip else tap
                weight.append(taps[tap : tap + 1, lanes])
            for r in rows:
                value = wide[ct, r, 5 + b : 5 + b + COLS, :]
                for a in range(KW):
                    if r - a in total:
                        total[r - a] = total[r - a] + value * weight[a]
        for j in hit:
            write(ct, lanes, j, total[j])
        return 0

    lax.fori_loop(0, 3, tile, 0)


def fold_into(edge, taps, read, write):
    def tile(ct, _):
        lanes = pl.ds(pl.multiple_of(ct * 128, 128), 128)
        total = [read(j, lanes) for j in range(3)]
        for b in range(KW):
            for j in range(3):
                for e in range(j + 1):
                    a = e + 6 - j
                    weight = taps[a * KW + b : a * KW + b + 1, lanes]
                    total[j] = total[j] + edge[ct, e, 5 + b : 5 + b + COLS, :] * weight
        for j in range(3):
            write(j, lanes, total[j])
        return 0

    lax.fori_loop(0, 3, tile, 0)


def fold_slots(p):
    q = jnp.where(p < 112, p - 96, p - 112)
    first = q // 3 * COLS + q % 3
    edge = jnp.where(q < 9, jnp.where(p < 112, first, first + COLS - 3), -1)
    return jnp.where(p < 96, p, edge)


def fold_cells(p):
    row, col = p // WIDE, p % WIDE
    west = 96 + (2 - row) * 3 + 7 - col
    east = 112 + (2 - row) * 3 + 42 - col
    inner = 95 - row * COLS - (col - 8)
    slot = jnp.where(col < 8, west, jnp.where(col < 40, inner, east))
    return jnp.where((col >= 5) & (col < 43), slot, -1)


def fold_swap(p):
    return p % 16 // 2 * 16 + p // 16 * 2 + p % 2


def body(
    state, cot, ocean, partner, taps_in, gain_in, shift_in, wup_in, bup_in, wdown_in, bdown_in, scale_in,
    gs_out, tile_out, small_out,
    xs, cs, oc, part, taps, gain, shift, wup0, bup0, wdown0, bdown, scale,
    hw, he, hv, cw, ce, dw, de, dv, ew, ee,
    wide, dwide, edge, acc, bacc, edge_rows, wup, wdown, bup,
    unit, rstd, normed, masked, dbr, dhid, pre, hidden, dpre, dnorm, dcv, dcb,
    g, gc, h, h1, h2, r2, t, tz, perm,
    s, sc, s1, sx, s2, sy, s3, sz, b1, b2, b3, fold,
    loc, hs, hr, qs, qr, ds, dr, es, er, cs_s, cs_r, f_s, f_r, k_s, k_r, z_s, z_r,
    sa_s, sa_r, sx_s, sx_r, sy_s, sy_r, sz_s, sz_r, gy_s, gy_r, gx_s, gx_r, gc_s, gc_r, fold_s, fold_r,
):
    ia, ja = lax.axis_index("ia"), lax.axis_index("ja")
    x, zl, c = ia // 16, lax.rem(ia // 2, 8), lax.rem(ia, 2)
    y, zh = ja // 2, lax.rem(ja, 2)
    z = zh * 8 + zl
    u = x * 2 + c
    top, bottom = ja == BANDS - 1, ja == 0
    east = {"ia": lax.rem(ia + 1, LANES), "ja": ja}
    west = {"ia": lax.rem(ia + LANES - 1, LANES), "ja": ja}
    north = {"ia": ia, "ja": ja + 1}
    south = {"ia": ia, "ja": ja - 1}

    def remote(src, dst, send, recv, device):
        return pltpu.make_async_remote_copy(
            src_ref=src, dst_ref=dst, send_sem=send, recv_sem=recv,
            device_id=device, device_id_type=pl.DeviceIdType.MESH,
        )

    def peer_x(d):
        return place(lax.rem(x + d, 4), y, z, c)

    def peer_y(d):
        return place(x, lax.rem(y + d, 4), z, c)

    def peer_z(d):
        return place(x, y, lax.rem(z + d, 16), c)

    def peer_u(d):
        to = lax.rem(u + d, 8)
        return {"ia": to // 2 * 16 + zl * 2 + lax.rem(to, 2), "ja": ja}

    def peer_v(d):
        return {"ia": x * 16 + lax.rem(zl + d, 8) * 2 + c, "ja": ja}

    other = place(x, y, z, 1 - c)

    loads = [
        pltpu.make_async_copy(src, dst, loc.at[i])
        for i, (src, dst) in enumerate(
            [
                (state, xs), (cot, cs), (ocean, oc), (taps_in, taps), (gain_in, gain), (shift_in, shift),
                (wup_in, wup0), (bup_in, bup0), (wdown_in, wdown0), (bdown_in, bdown), (scale_in, scale),
                (partner, part),
            ]
        )
    ]
    for load in loads:
        load.start()

    barrier = pltpu.get_barrier_semaphore()

    def greet(device):
        pl.semaphore_signal(barrier, inc=1, device_id=device, device_id_type=pl.DeviceIdType.MESH)

    greet({"ia": ia, "ja": lax.rem(ja + 1, BANDS)})
    greet({"ia": ia, "ja": lax.rem(ja + BANDS - 1, BANDS)})
    greet(east)
    greet(west)

    @pl.when(top)
    def _():
        for d in range(1, 8):
            greet(peer_u(d))
            greet(peer_v(d))

    for d in range(1, 16):
        greet(peer_z(d))
    for d in range(1, 4):
        greet(peer_x(d))
        greet(peer_y(d))
    greet(other)

    for load in loads:
        load.wait()

    def old(p):
        return (p % 384) // 96 * 192 + (p % 96) // 12 * 24 + p // 384 * 12 + p % 12

    perm[...] = onehot(HID, HID, old)
    wup[...] = dot(wup0[...], perm[...]).astype(BF16)
    wdown[...] = dot(wdown0[...], perm[...]).astype(BF16)
    bup[...] = jnp.sum(dot(split3(bup0[...][None]), perm[...]), axis=0, keepdims=True)

    eye = (
        lax.broadcasted_iota(jnp.int32, (COLS, COLS), 0)
        == lax.broadcasted_iota(jnp.int32, (COLS, COLS), 1)
    ).astype(F32)

    def mask_row(j, total):
        sea = jnp.sum(eye * oc[pl.ds(j, 1), :].astype(F32), axis=1, keepdims=True)
        cells = pl.ds(pl.multiple_of(j * COLS, COLS), COLS)
        value = cs[j].astype(F32) * sea
        masked[cells, :] = value
        dbr[cells, :] = (value * scale[...][None]).astype(BF16)
        return total + sub8(value * scale[...][None])

    g_bdown = lax.fori_loop(0, ROWS, mask_row, jnp.zeros((8, CH), F32))
    dhid[...] = dot(dbr[...], wdown[...])

    def widen_own(dst, centre):
        for ct in range(3):
            lanes = slice(ct * 128, ct * 128 + 128)
            for r in range(ROWS):
                dst[ct, PAD + r, 8:40, :] = centre[r, :, lanes].astype(F32)

    def widen_sides(dst, w, e):
        for ct in range(3):
            lanes = slice(ct * 128, ct * 128 + 128)
            for r in range(ROWS):
                dst[ct, PAD + r, 0:8, :] = w[r, :, lanes].astype(F32)[8:16]
                dst[ct, PAD + r, 40:48, :] = e[r, :, lanes].astype(F32)[0:8]

    def widen_rows(dst, v, k):
        for ct in range(3):
            lanes = slice(ct * 128, ct * 128 + 128)
            for q in range(PAD):
                dst[ct, q + k * (ROWS + PAD), 8:40, :] = v[k, q, :, lanes].astype(F32)

    def widen_corners(dst, w, e, k):
        for ct in range(3):
            lanes = slice(ct * 128, ct * 128 + 128)
            for q in range(PAD):
                dst[ct, q + k * (ROWS + PAD), 0:8, :] = w[k, q, :, lanes].astype(F32)[8:16]
                dst[ct, q + k * (ROWS + PAD), 40:48, :] = e[k, q, :, lanes].astype(F32)[0:8]

    widen_own(wide, xs)

    def fold_copies(k, step, peer, me):
        return [
            remote(
                fold.at[k, step, 0, lax.rem(me + d, 8)], fold.at[k, step, 1, me],
                fold_s.at[k, step, d - 1], fold_r.at[k, step, d - 1], peer(d),
            )
            for d in range(1, 8)
        ]

    fold_steps = ((peer_u, u), (peer_v, zl), (peer_v, zl), (peer_u, u))

    def fold_put(k, step, value):
        fold[k, step, 0] = value.astype(BF16).reshape(8, 16, CH)

    def fold_start(k, step):
        peer, me = fold_steps[step]
        for copy in fold_copies(k, step, peer, me):
            copy.start()
        fold[k, step, 1, me] = fold[k, step, 0, me]

    def fold_send(k, step, value):
        fold_put(k, step, value)
        fold_start(k, step)

    def fold_take(k, step):
        peer, me = fold_steps[step]
        for copy in fold_copies(k, step, peer, me):
            copy.wait()
        return fold[k, step, 1].reshape(128, CH)

    def fold_first(k, strip):
        fold_put(k, 0, dot(onehot(96, 128, fold_slots), strip, (0, 0)))

    def fold_next(k, step):
        value = fold_take(k, step - 1)

        def facing(p):
            into = p % 16 // 2
            target = into // 2 * 16 + p // 16 * 2 + into % 2
            shift = jnp.where(u == 6, 1, 0) - jnp.where(u == 7, 1, 0)
            source = (part[...] + ia - target + shift + LANES) % LANES
            return source // 2 % 8 * 16 + (source // 16 * 2 + source % 2) * 2 + p % 2

        matrix = onehot(128, 128, facing if step == 2 else fold_swap)
        fold_send(k, step, dot(matrix, value, (0, 0)))

    def fold_last(k):
        return dot(onehot(128, PAD * WIDE, fold_cells), fold_take(k, 3), (0, 0))

    @pl.when(top)
    def _():
        fold_first(0, xs[4:7].reshape(96, CH))

    pl.semaphore_wait(barrier, 26 + jnp.where(top, 14, 0))

    def halo(src, w, e, v, send, recv):
        return (
            remote(src.at[5:8], v.at[0], send.at[0], recv.at[0], north),
            remote(src.at[0:3], v.at[1], send.at[1], recv.at[1], south),
            remote(src.at[:, 16:32], w, send.at[2], recv.at[2], east),
            remote(src.at[:, 0:16], e, send.at[3], recv.at[3], west),
        )

    def start_south(copies):
        @pl.when(jnp.logical_not(bottom))
        def _():
            copies[1].start()

    def start_rest(copies):
        @pl.when(jnp.logical_not(top))
        def _():
            copies[0].start()

        copies[2].start()
        copies[3].start()

    def finish_south(copies):
        @pl.when(jnp.logical_not(bottom))
        def _():
            copies[1].wait_send()
            copies[0].wait_recv()

    def finish_north(copies):
        @pl.when(jnp.logical_not(top))
        def _():
            copies[0].wait_send()
            copies[1].wait_recv()

    def corners(v, w, e, send, recv):
        copies = []
        for k in range(2):
            copies.append(remote(v.at[k, :, 16:32], w.at[k], send.at[2 * k], recv.at[2 * k], east))
            copies.append(remote(v.at[k, :, 0:16], e.at[k], send.at[2 * k + 1], recv.at[2 * k + 1], west))
        return copies

    def rows_arrived(dst, copies, v, w, e, send, recv):
        passed = corners(v, w, e, send, recv)
        finish_south(copies)
        passed[0].start()
        passed[1].start()
        widen_rows(dst, v, 0)
        finish_north(copies)

        @pl.when(jnp.logical_not(top))
        def _():
            passed[2].start()
            passed[3].start()
            widen_rows(dst, v, 1)

        return passed

    def finish_corners_south(dst, copies, w, e):
        copies[0].wait()
        copies[1].wait()
        widen_corners(dst, w, e, 0)

    def finish_corners_north(dst, copies, w, e):
        @pl.when(jnp.logical_not(top))
        def _():
            copies[2].wait()
            copies[3].wait()
            widen_corners(dst, w, e, 1)

    first = halo(state, hw, he, hv, hs, hr)

    @pl.when(top)
    def _():
        fold_start(0, 0)

    start_south(first)
    start_rest(first)

    @pl.when(top)
    def _():
        fold_next(0, 1)

    @pl.when(bottom)
    def _():
        hv[0] = jnp.zeros((PAD, COLS, CH), BF16)

    own, south_rows, north_rows = tuple(range(PAD, PAD + ROWS)), (0, 1, 2), (11, 12, 13)
    every = tuple(range(ROWS))

    def nothing(ct, j):
        return jnp.zeros((COLS, 128), F32)

    def read_acc(ct, j):
        return acc[ct, j]

    def write_acc(ct, lanes, j, value):
        acc[ct, j] = value

    for copy in first[2:]:
        copy.wait()
    widen_sides(wide, hw, he)
    conv_part(wide, taps, False, own, every, nothing, write_acc)

    @pl.when(top)
    def _():
        fold_next(0, 2)

    second = rows_arrived(wide, first, hv, cw, ce, qs, qr)

    @pl.when(top)
    def _():
        fold_next(0, 3)

    def half_pass(k):
        base = k * 128
        block = slice(base, base + 128)
        beyond = (south_rows, north_rows)[k]
        conv_part(wide, taps, False, beyond, every[4 * k : 4 * k + 4], read_acc, write_acc)

        def norm_rows(i, _):
            cells = pl.ds(pl.multiple_of(base + i * 32, 32), 32)
            value = jnp.concatenate([acc[ct, 4 * k + i] for ct in range(3)], axis=1)
            value = value - jnp.mean(value, axis=1, keepdims=True)
            r = lax.rsqrt(jnp.mean(value * value, axis=1, keepdims=True) + 1e-06)
            value = value * r
            rstd[cells, :] = r
            unit[cells, :] = value
            normed[cells, :] = (value * gain[...][None] + shift[...][None]).astype(BF16)
            return 0

        lax.fori_loop(0, 4, norm_rows, 0, unroll=True)
        pre[...] = dot(normed[block, :], wup[...])

        def gelu_rows(i, totals):
            here = pl.ds(pl.multiple_of(i * 32, 32), 32)
            cells = pl.ds(pl.multiple_of(base + i * 32, 32), 32)
            done = []
            for q in range(3):
                lanes = slice(q * 256, q * 256 + 256)
                v = pre[here, lanes] + bup[:, lanes]
                square = v * v
                tanh = jnp.tanh(v * (COEFF + COEFF * CUBIC * square))
                half = 0.5 + 0.5 * tanh
                value = v * half
                slope = half + value * (1.0 - tanh) * (COEFF + 3.0 * CUBIC * COEFF * square)
                hidden[cells, lanes] = value.astype(BF16)
                grad = dhid[cells, lanes] * slope
                dpre[cells, lanes] = grad.astype(BF16)
                done.append(totals[q] + sub8(grad))
            return tuple(done)

        bias = lax.fori_loop(0, 4, gelu_rows, tuple(jnp.zeros((8, 256), F32) for _ in range(3)), unroll=2)
        dnorm[...] = dot(dpre[block, :], wup[...], (1, 1))

        def back_rows(i, totals):
            here = pl.ds(pl.multiple_of(i * 32, 32), 32)
            cells = pl.ds(pl.multiple_of(base + i * 32, 32), 32)
            unit_rows = unit[cells, :]
            grad = dnorm[here, :]
            product = grad * unit_rows
            scaled = grad * gain[...][None]
            mean_a = jnp.mean(scaled, axis=1, keepdims=True)
            mean_b = jnp.mean(product * gain[...][None], axis=1, keepdims=True)
            value = rstd[cells, :] * (scaled - mean_a - unit_rows * mean_b)
            value = value.astype(BF16)
            dcb[4 * k + i] = value
            value = value.astype(F32)
            for ct in range(3):
                dcv[ct, 4 * k + i] = value[:, ct * 128 : ct * 128 + 128]
            return totals[0] + sub8(product), totals[1] + sub8(grad)

        zero = jnp.zeros((8, CH), F32)
        return bias, lax.fori_loop(0, 4, back_rows, (zero, zero), unroll=True)

    @pl.when(bottom)
    def _():
        dv[0] = jnp.zeros((PAD, COLS, CH), BF16)

    finish_corners_south(wide, second, cw, ce)
    bias_a, norm_a = half_pass(0)
    third = halo(dcb, dw, de, dv, ds, dr)
    start_south(third)

    finish_corners_north(wide, second, cw, ce)

    @pl.when(top)
    def _():
        ghost = fold_last(0)
        for ct in range(3):
            for q in range(PAD):
                wide[ct, ROWS + PAD + q] = ghost[q * WIDE : (q + 1) * WIDE, ct * 128 : ct * 128 + 128]

    bias_b, norm_b = half_pass(1)

    start_rest(third)

    @pl.when(top)
    def _():
        fold_first(1, dcb[5:8].reshape(96, CH))
        fold_start(1, 0)

    def tap_tile(ct, _):
        lanes = pl.ds(pl.multiple_of(ct * 128, 128), 128)
        for b in range(KW):
            total = [jnp.zeros((8, 128), F32) for _ in range(KW)]
            for r in range(ROWS + 2 * PAD):
                value = wide[ct, r, 5 + b : 5 + b + COLS, :]
                for a in range(KW):
                    j = r - a
                    if 0 <= j < ROWS:
                        total[a] = total[a] + sub8(value * dcv[ct, j])
            for a in range(KW):
                s[a * KW + b : a * KW + b + 1, lanes] = jnp.sum(total[a], axis=0, keepdims=True)
        return 0

    s[...] = jnp.zeros((64, 512), F32)
    lax.fori_loop(0, 3, tap_tile, 0)

    branch = dot(hidden[...], wdown[...], (1, 1)) + bdown[...][None]
    g_scale = jnp.sum(masked[...] * branch, axis=0, keepdims=True)
    g_bup = jnp.concatenate(
        [jnp.sum(va + vb, axis=0, keepdims=True) for va, vb in zip(bias_a, bias_b)], axis=1
    )
    back = jnp.sum(dot(split3(g_bup), perm[...], (1, 1)), axis=0, keepdims=True)
    s[49:50, 0:CH] = jnp.sum(norm_a[0] + norm_b[0], axis=0, keepdims=True)
    s[50:51, 0:CH] = jnp.sum(norm_a[1] + norm_b[1], axis=0, keepdims=True)
    s[51:52, 0:CH] = jnp.sum(g_bdown, axis=0, keepdims=True)
    s[52:53, 0:CH] = g_scale
    s[53:54, 0:CH] = back[:, 0:CH]
    s[54:55, 0:CH] = back[:, CH:HID]
    half_s = pl.multiple_of((1 - c) * 32, 32)
    cross_s = remote(s.at[pl.ds(half_s, 32)], sc, sa_s.at[0], sa_r.at[0], other)
    cross_s.start()

    for half in range(2):
        units = slice(half * 384, half * 384 + 384)
        g[0, half] = dot(dpre[:, units], normed[...], (0, 0)).astype(BF16)
        g[1, half] = dot(dbr[...], hidden[:, units], (0, 0)).astype(BF16)
    cross = remote(g.at[:, 1 - c], gc, cs_s.at[0], cs_r.at[0], other)
    cross.start()

    cross_s.wait()
    mine_s = pl.multiple_of(c * 32, 32)
    s1[...] = (s[pl.ds(mine_s, 32), :] + sc[...]).reshape(4, 8, 512)
    small = []
    for d in range(1, 4):
        copy = remote(s1.at[lax.rem(x + d, 4)], sx.at[d - 1], sx_s.at[d - 1], sx_r.at[d - 1], peer_x(d))
        copy.start()
        small.append(copy)

    cross.wait()
    for k in range(2):
        for q in range(4):
            rows = slice(q * 96, q * 96 + 96)
            h[k, q] = (g[k, c, rows, :].astype(F32) + gc[k, rows, :].astype(F32)).astype(BF16)
    along = []
    for d in range(1, 4):
        up = remote(h.at[0, lax.rem(x + d, 4)], h1.at[0, d - 1], f_s.at[0, d - 1], f_r.at[0, d - 1], peer_x(d))
        down = remote(h.at[1, lax.rem(y + d, 4)], h1.at[1, d - 1], f_s.at[1, d - 1], f_r.at[1, d - 1], peer_y(d))
        up.start()
        down.start()
        along += [up, down]

    @pl.when(top)
    def _():
        fold_next(1, 1)

    def put_back(ct, lanes, j, value):
        value = cs[j, :, lanes].astype(F32) + value
        gs_out[j, :, lanes] = value.astype(BF16)
        if 4 <= j < 7:
            edge_rows[j - 4, :, lanes] = value

    def write_bacc(ct, lanes, j, value):
        if 3 <= j < 5:
            put_back(ct, lanes, j, value)
        else:
            bacc[ct, j] = value

    def read_bacc(ct, j):
        return bacc[ct, j]

    widen_own(dwide, dcb)

    for copy in small:
        copy.wait()
    s2[...] = s1[x] + sx[0] + sx[1] + sx[2]
    small = []
    for d in range(1, 4):
        chunk = pl.ds(pl.multiple_of(lax.rem(y + d, 4) * 128, 128), 128)
        copy = remote(s2.at[:, chunk], sy.at[d - 1], sy_s.at[d - 1], sy_r.at[d - 1], peer_y(d))
        copy.start()
        small.append(copy)

    for copy in third[2:]:
        copy.wait()
    widen_sides(dwide, dw, de)
    conv_part(dwide, taps, True, own, every, nothing, write_bacc)

    for copy in small:
        copy.wait()
    mine_y = pl.ds(pl.multiple_of(y * 128, 128), 128)
    s3[...] = s2[:, mine_y] + sy[0] + sy[1] + sy[2]
    small = []
    for d in range(1, 16):
        copy = remote(s3, sz.at[z], sz_s.at[d - 1], sz_r.at[d - 1], peer_z(d))
        copy.start()
        small.append(copy)
    sz[z] = s3[...]

    for copy in along:
        copy.wait()
    spread = onehot(CH, 512, lambda p: jnp.where(p % 128 < 96, p // 128 * 96 + p % 128, -1))
    for k in range(2):
        mine = h[k, (x, y)[k]].astype(F32)
        mine = mine + h1[k, 0].astype(F32) + h1[k, 1].astype(F32) + h1[k, 2].astype(F32)
        mine = dot(mine.astype(BF16), spread).astype(BF16)
        for q in range(4):
            h2[k, q] = mine[:, q * 128 : q * 128 + 128]
    along = []
    for d in range(1, 4):
        up = remote(h2.at[0, lax.rem(y + d, 4)], r2.at[0, d - 1], k_s.at[0, d - 1], k_r.at[0, d - 1], peer_y(d))
        down = remote(h2.at[1, lax.rem(x + d, 4)], r2.at[1, d - 1], k_s.at[1, d - 1], k_r.at[1, d - 1], peer_x(d))
        up.start()
        down.start()
        along += [up, down]

    for copy in along:
        copy.wait()
    parts = []
    for k in range(2):
        mine = h2[k, (y, x)[k]].astype(F32)
        mine = mine + r2[k, 0].astype(F32) + r2[k, 1].astype(F32) + r2[k, 2].astype(F32)
        parts.append(mine.astype(BF16))
    pick_up = onehot(128, 256, lambda p: jnp.where(p % 128 < 48, p // 128 * 48 + p % 128, -1))
    pick_down = onehot(
        96, 256, lambda p: jnp.where((p % 128 >= 64) & (p % 128 < 112), p // 128 * 48 + p % 128 - 64, -1)
    )
    both = dot(parts[0], pick_up) + dot(parts[1], pick_down, (0, 0))[0:96]
    rows_to = onehot(96, 128, lambda p: jnp.where(p % 16 < 12, p // 16 * 12 + p % 16, -1))
    tiles = dot(rows_to, both.astype(BF16), (0, 0)).astype(BF16)
    for q in range(16):
        t[q] = tiles[q % 8 * 16 : q % 8 * 16 + 16, q // 8 * 128 : q // 8 * 128 + 128]
    along = []
    for d in range(1, 16):
        copy = remote(t.at[lax.rem(z + d, 16)], tz.at[d - 1], z_s.at[d - 1], z_r.at[d - 1], peer_z(d))
        copy.start()
        along.append(copy)

    @pl.when(top)
    def _():
        fold_next(1, 2)

    for copy in small:
        copy.wait()
    total = sz[0]
    for q in range(1, 16):
        total = total + sz[q]
    b1[:, mine_y] = total * FACTOR
    gather = []
    for d in range(1, 4):
        copy = remote(b1.at[:, mine_y], b1.at[:, mine_y], gy_s.at[d - 1], gy_r.at[d - 1], peer_y(d))
        copy.start()
        gather.append(copy)

    fourth = rows_arrived(dwide, third, dv, ew, ee, es, er)

    @pl.when(top)
    def _():
        dwide[:, ROWS + PAD :] = jnp.zeros((3, PAD, WIDE, 128), F32)

    for copy in gather:
        copy.wait()
    b2[x] = b1[...]
    gather = []
    for d in range(1, 4):
        copy = remote(b1, b2.at[x], gx_s.at[d - 1], gx_r.at[d - 1], peer_x(d))
        copy.start()
        gather.append(copy)

    @pl.when(top)
    def _():
        fold_next(1, 3)

    finish_corners_south(dwide, fourth, ew, ee)
    finish_corners_north(dwide, fourth, ew, ee)
    conv_part(dwide, taps, True, south_rows + north_rows, every, read_bacc, put_back)

    for copy in gather:
        copy.wait()
    b3[c] = b2[...]
    last = remote(b2, b3.at[c], gc_s.at[0], gc_r.at[0], other)
    last.start()

    for copy in along:
        copy.wait()
    total = t[z].astype(F32)
    for d in range(15):
        total = total + tz[d].astype(F32)
    tile_out[...] = total * FACTOR

    @pl.when(top)
    def _():
        ghost = fold_last(1)
        for ct in range(3):
            for q in range(PAD):
                edge[ct, q] = ghost[q * WIDE : (q + 1) * WIDE, ct * 128 : ct * 128 + 128]

        def read_edge(j, lanes):
            return edge_rows[j, :, lanes]

        def put_edge(j, lanes, value):
            gs_out[4 + j, :, lanes] = value.astype(BF16)

        fold_into(edge, taps, read_edge, put_edge)

    last.wait()
    small_out[...] = b3[...].reshape(64, 512)


def finish(gs_in, tile_in, small_in, gs_out, up_out, down_out, gk_out, gc_out, gb_out):
    gs_out[...] = gs_in[...]
    up_out[...] = tile_in[0:12, 0:48]
    down_out[...] = tile_in[0:12, 64:112]
    gk_out[...] = small_in[0:49, 0:CH]
    gc_out[...] = small_in[49:53, 0:CH]
    gb_out[0:CH] = small_in[53, 0:CH]
    gb_out[CH:HID] = small_in[54, 0:CH]


def fused(*args):
    sds = jax.ShapeDtypeStruct
    vm = pltpu.VMEM
    dma = pltpu.SemaphoreType.DMA
    hbm_spec = pl.BlockSpec(memory_space=pltpu.HBM)
    vm_spec = pl.BlockSpec(memory_space=pltpu.VMEM)
    edge16 = (ROWS, 16, CH)
    corner = (2, PAD, 16, CH)
    scratch = [
        vm((ROWS, COLS, CH), BF16), vm((ROWS, COLS, CH), BF16), vm((ROWS, COLS), jnp.int32), vm((1, 1), jnp.int32),
        vm((49, CH), F32), vm((CH,), F32), vm((CH,), F32), vm((CH, HID), BF16), vm((HID,), F32),
        vm((CH, HID), BF16), vm((CH,), F32), vm((CH,), F32),
        vm(edge16, BF16), vm(edge16, BF16), vm((2, PAD, COLS, CH), BF16), vm(corner, BF16), vm(corner, BF16),
        vm(edge16, BF16), vm(edge16, BF16), vm((2, PAD, COLS, CH), BF16), vm(corner, BF16), vm(corner, BF16),
        vm((3, 14, WIDE, 128), F32), vm((3, 14, WIDE, 128), F32), vm((3, PAD, WIDE, 128), F32),
        vm((3, ROWS, COLS, 128), F32), vm((3, ROWS, COLS, 128), F32), vm((PAD, COLS, CH), F32),
        vm((CH, HID), BF16), vm((CH, HID), BF16), vm((1, HID), F32),
        vm((CELLS, CH), F32), vm((CELLS, 1), F32), vm((CELLS, CH), BF16),
        vm((CELLS, CH), F32), vm((CELLS, CH), BF16), vm((CELLS, HID), F32), vm((CELLS // 2, HID), F32),
        vm((CELLS, HID), BF16), vm((CELLS, HID), BF16), vm((CELLS // 2, CH), F32),
        vm((3, ROWS, COLS, 128), F32), vm((ROWS, COLS, CH), BF16),
        vm((2, 2, 384, 384), BF16), vm((2, 384, 384), BF16), vm((2, 4, 96, 384), BF16),
        vm((2, 3, 96, 384), BF16), vm((2, 4, 96, 128), BF16), vm((2, 3, 96, 128), BF16),
        vm((16, 16, 128), BF16), vm((15, 16, 128), BF16), vm((HID, HID), BF16),
        vm((64, 512), F32), vm((32, 512), F32), vm((4, 8, 512), F32), vm((3, 8, 512), F32), vm((8, 512), F32),
        vm((3, 8, 128), F32), vm((8, 128), F32), vm((16, 8, 128), F32), vm((8, 512), F32), vm((4, 8, 512), F32),
        vm((2, 4, 8, 512), F32), vm((2, 4, 2, 8, 16, CH), BF16),
        dma((12,)), dma((4,)), dma((4,)), dma((4,)), dma((4,)), dma((4,)), dma((4,)), dma((4,)), dma((4,)),
        dma((1,)), dma((1,)), dma((2, 3)), dma((2, 3)), dma((2, 3)), dma((2, 3)), dma((15,)), dma((15,)),
        dma((1,)), dma((1,)), dma((3,)), dma((3,)), dma((3,)), dma((3,)), dma((15,)), dma((15,)),
        dma((3,)), dma((3,)), dma((3,)), dma((3,)), dma((1,)), dma((1,)), dma((2, 4, 7)), dma((2, 4, 7)),
    ]
    return pl.pallas_call(
        body,
        out_shape=[sds((ROWS, COLS, CH), BF16), sds((16, 128), F32), sds((64, 512), F32)],
        in_specs=[hbm_spec] * 12,
        out_specs=[vm_spec] * 3,
        scratch_shapes=scratch,
        compiler_params=pltpu.CompilerParams(
            collective_id=0, has_side_effects=True, vmem_limit_bytes=63 * 2**20
        ),
        name="block",
    )(*args)


def local(
    state, cotangent, ocean, fold_partner, kernel, ln_gain, ln_shift, w_up, b_up, w_down, b_down, layer_scale
):
    results = fused(
        state, cotangent, ocean, fold_partner[None], kernel, ln_gain, ln_shift, w_up, b_up,
        w_down, b_down, layer_scale,
    )
    sds = jax.ShapeDtypeStruct
    grad_state, up, down, g_kernel, g_chan, g_bup = (
        pl.pallas_call(
            finish,
            out_shape=[
                sds((ROWS, COLS, CH), BF16), sds((12, 48), F32), sds((12, 48), F32),
                sds((49, CH), F32), sds((4, CH), F32), sds((HID,), F32),
            ],
            name="outputs",
        )(*results)
    )
    return grad_state, up.T, down.T, g_kernel, g_chan, g_bup


def solution(mesh):
    placed = (P("ja", "ia", None), P("ja", "ia", None), P("ja", "ia"), P("ia")) + (P(),) * 8
    return jax.shard_map(
        local,
        mesh=mesh,
        in_specs=placed,
        out_specs=(P("ja", "ia", None), P("ja", "ia"), P("ja", "ia"), P(), P(), P()),
        check_vma=False,
    )
```

```python
import functools
import math

import jax
import jax.numpy as jnp
from jax import lax
from jax.experimental import pallas as pl
from jax.experimental.pallas import tpu as pltpu
from jax.sharding import PartitionSpec as P

KW = 7
PAD = 3
ROWS = 8
COLS = 32
CH = 384
HID = 768
CELLS = ROWS * COLS
WIDE = 48
F32 = jnp.float32
BF16 = jnp.bfloat16
LANES = 64
BANDS = 8
COEFF = 0.7978845608028654
CUBIC = 0.044715
FACTOR = 1.0 / math.sqrt(ROWS * BANDS * COLS * LANES)


def place(x, y, z, c):
    return {"ia": x * 16 + lax.rem(z, 8) * 2 + c, "ja": y * 2 + z // 8}


def dot(a, b, dims=(1, 0)):
    return lax.dot_general(
        a, b, (((dims[0],), (dims[1],)), ((), ())), preferred_element_type=F32
    )


def sub8(v):
    return v[0:8] + v[8:16] + v[16:24] + v[24:32]


def onehot(rows, cols, target):
    want = target(lax.broadcasted_iota(jnp.int32, (1, cols), 1))
    here = lax.broadcasted_iota(jnp.int32, (rows, cols), 0)
    return jnp.where(here == want, 1.0, 0.0).astype(BF16)


def split3(v):
    hi = v.astype(BF16)
    rest = v - hi.astype(F32)
    mid = rest.astype(BF16)
    low = (rest - mid.astype(F32)).astype(BF16)
    zeros = jnp.zeros((13, v.shape[1]), F32)
    return jnp.concatenate(
        [hi.astype(F32), mid.astype(F32), low.astype(F32), zeros], axis=0
    ).astype(BF16)


def conv_part(wide, taps, flip, rows, outs, read, write):
    def tile(ct, _):
        lanes = pl.ds(pl.multiple_of(ct * 128, 128), 128)
        hit = [j for j in outs if any(0 <= r - j < KW for r in rows)]
        total = {j: read(ct, j) for j in hit}
        for b in range(KW):
            weight = []
            for a in range(KW):
                tap = a * KW + b
                tap = KW * KW - 1 - tap if flip else tap
                weight.append(taps[tap : tap + 1, lanes])
            for r in rows:
                value = wide[ct, r, 5 + b : 5 + b + COLS, :]
                for a in range(KW):
                    if r - a in total:
                        total[r - a] = total[r - a] + value * weight[a]
        for j in hit:
            write(ct, lanes, j, total[j])
        return 0

    lax.fori_loop(0, 3, tile, 0)


def fold_into(edge, taps, read, write):
    def tile(ct, _):
        lanes = pl.ds(pl.multiple_of(ct * 128, 128), 128)
        total = [read(j, lanes) for j in range(3)]
        for b in range(KW):
            for j in range(3):
                for e in range(j + 1):
                    a = e + 6 - j
                    weight = taps[a * KW + b : a * KW + b + 1, lanes]
                    total[j] = total[j] + edge[ct, e, 5 + b : 5 + b + COLS, :] * weight
        for j in range(3):
            write(j, lanes, total[j])
        return 0

    lax.fori_loop(0, 3, tile, 0)


def fold_slots(p):
    q = jnp.where(p < 112, p - 96, p - 112)
    first = q // 3 * COLS + q % 3
    edge = jnp.where(q < 9, jnp.where(p < 112, first, first + COLS - 3), -1)
    return jnp.where(p < 96, p, edge)


def fold_cells(p):
    row, col = p // WIDE, p % WIDE
    west = 96 + (2 - row) * 3 + 7 - col
    east = 112 + (2 - row) * 3 + 42 - col
    inner = 95 - row * COLS - (col - 8)
    slot = jnp.where(col < 8, west, jnp.where(col < 40, inner, east))
    return jnp.where((col >= 5) & (col < 43), slot, -1)


def fold_swap(p):
    return p % 16 // 2 * 16 + p // 16 * 2 + p % 2


def body(
    state, cot, ocean, partner, taps_in, gain_in, shift_in, wup_in, bup_in, wdown_in, bdown_in, scale_in,
    gs_out, tile_out, small_out,
    xs, cs, oc, part, taps, gain, shift, wup0, bup0, wdown0, bdown, scale,
    hw, he, hv, cw, ce, dw, de, dv, ew, ee,
    wide, dwide, edge, acc, bacc, edge_rows, wup, wdown, bup,
    unit, rstd, normed, masked, dbr, dhid, pre, hidden, dpre, dnorm, dcv, dcb,
    g, gc, h, h1, h2, r2, t, tz, perm,
    s, sc, s1, sx, s3, sz, b2, b3, fold,
    loc, hs, hr, qs, qr, ds, dr, es, er, cs_s, cs_r, f_s, f_r, k_s, k_r, z_s, z_r,
    sa_s, sa_r, sx_s, sx_r, sz_s, sz_r, gx_s, gx_r, gc_s, gc_r, fold_s, fold_r,
):
    ia, ja = lax.axis_index("ia"), lax.axis_index("ja")
    x, zl, c = ia // 16, lax.rem(ia // 2, 8), lax.rem(ia, 2)
    y, zh = ja // 2, lax.rem(ja, 2)
    z = zh * 8 + zl
    u = x * 2 + c
    top, bottom = ja == BANDS - 1, ja == 0
    east = {"ia": lax.rem(ia + 1, LANES), "ja": ja}
    west = {"ia": lax.rem(ia + LANES - 1, LANES), "ja": ja}
    north = {"ia": ia, "ja": ja + 1}
    south = {"ia": ia, "ja": ja - 1}

    def remote(src, dst, send, recv, device):
        return pltpu.make_async_remote_copy(
            src_ref=src, dst_ref=dst, send_sem=send, recv_sem=recv,
            device_id=device, device_id_type=pl.DeviceIdType.MESH,
        )

    def peer_x(d):
        return place(lax.rem(x + d, 4), y, z, c)

    def peer_y(d):
        return place(x, lax.rem(y + d, 4), z, c)

    def peer_z(d):
        return place(x, y, lax.rem(z + d, 16), c)

    def peer_xy(d):
        return place(lax.rem(x + d // 4, 4), lax.rem(y + d % 4, 4), z, c)

    def peer_u(d):
        to = lax.rem(u + d, 8)
        return {"ia": to // 2 * 16 + zl * 2 + lax.rem(to, 2), "ja": ja}

    def peer_v(d):
        return {"ia": x * 16 + lax.rem(zl + d, 8) * 2 + c, "ja": ja}

    other = place(x, y, z, 1 - c)

    loads = [
        pltpu.make_async_copy(src, dst, loc.at[i])
        for i, (src, dst) in enumerate(
            [
                (state, xs), (cot, cs), (ocean, oc), (taps_in, taps), (gain_in, gain), (shift_in, shift),
                (wup_in, wup0), (bup_in, bup0), (wdown_in, wdown0), (bdown_in, bdown), (scale_in, scale),
                (partner, part),
            ]
        )
    ]
    for load in loads:
        load.start()

    barrier = pltpu.get_barrier_semaphore()

    def greet(device):
        pl.semaphore_signal(barrier, inc=1, device_id=device, device_id_type=pl.DeviceIdType.MESH)

    greet({"ia": ia, "ja": lax.rem(ja + 1, BANDS)})
    greet({"ia": ia, "ja": lax.rem(ja + BANDS - 1, BANDS)})
    greet(east)
    greet(west)

    @pl.when(top)
    def _():
        for d in range(1, 8):
            greet(peer_u(d))
            greet(peer_v(d))

    for d in range(1, 16):
        greet(peer_z(d))
    for d in range(1, 16):
        greet(peer_xy(d))
    greet(other)

    for load in loads:
        load.wait()

    def old(p):
        return (p % 384) // 96 * 192 + (p % 96) // 12 * 24 + p // 384 * 12 + p % 12

    perm[...] = onehot(HID, HID, old)
    wup[...] = dot(wup0[...], perm[...]).astype(BF16)
    wdown[...] = dot(wdown0[...], perm[...]).astype(BF16)
    bup[...] = jnp.sum(dot(split3(bup0[...][None]), perm[...]), axis=0, keepdims=True)

    eye = (
        lax.broadcasted_iota(jnp.int32, (COLS, COLS), 0)
        == lax.broadcasted_iota(jnp.int32, (COLS, COLS), 1)
    ).astype(F32)

    def mask_row(j, total):
        sea = jnp.sum(eye * oc[pl.ds(j, 1), :].astype(F32), axis=1, keepdims=True)
        cells = pl.ds(pl.multiple_of(j * COLS, COLS), COLS)
        value = cs[j].astype(F32) * sea
        masked[cells, :] = value
        dbr[cells, :] = (value * scale[...][None]).astype(BF16)
        return total + sub8(value * scale[...][None])

    g_bdown = lax.fori_loop(0, ROWS, mask_row, jnp.zeros((8, CH), F32))
    dhid[...] = dot(dbr[...], wdown[...])

    def widen_own(dst, centre):
        for ct in range(3):
            lanes = slice(ct * 128, ct * 128 + 128)
            for r in range(ROWS):
                dst[ct, PAD + r, 8:40, :] = centre[r, :, lanes].astype(F32)

    def widen_sides(dst, w, e):
        for ct in range(3):
            lanes = slice(ct * 128, ct * 128 + 128)
            for r in range(ROWS):
                dst[ct, PAD + r, 0:8, :] = w[r, :, lanes].astype(F32)[8:16]
                dst[ct, PAD + r, 40:48, :] = e[r, :, lanes].astype(F32)[0:8]

    def widen_rows(dst, v, k):
        for ct in range(3):
            lanes = slice(ct * 128, ct * 128 + 128)
            for q in range(PAD):
                dst[ct, q + k * (ROWS + PAD), 8:40, :] = v[k, q, :, lanes].astype(F32)

    def widen_corners(dst, w, e, k):
        for ct in range(3):
            lanes = slice(ct * 128, ct * 128 + 128)
            for q in range(PAD):
                dst[ct, q + k * (ROWS + PAD), 0:8, :] = w[k, q, :, lanes].astype(F32)[8:16]
                dst[ct, q + k * (ROWS + PAD), 40:48, :] = e[k, q, :, lanes].astype(F32)[0:8]

    widen_own(wide, xs)

    def fold_copies(k, step, peer, me):
        return [
            remote(
                fold.at[k, step, 0, lax.rem(me + d, 8)], fold.at[k, step, 1, me],
                fold_s.at[k, step, d - 1], fold_r.at[k, step, d - 1], peer(d),
            )
            for d in range(1, 8)
        ]

    fold_steps = ((peer_u, u), (peer_v, zl), (peer_v, zl), (peer_u, u))

    def fold_put(k, step, value):
        fold[k, step, 0] = value.astype(BF16).reshape(8, 16, CH)

    def fold_start(k, step):
        peer, me = fold_steps[step]
        for copy in fold_copies(k, step, peer, me):
            copy.start()
        fold[k, step, 1, me] = fold[k, step, 0, me]

    def fold_send(k, step, value):
        fold_put(k, step, value)
        fold_start(k, step)

    def fold_take(k, step):
        peer, me = fold_steps[step]
        for copy in fold_copies(k, step, peer, me):
            copy.wait()
        return fold[k, step, 1].reshape(128, CH)

    def fold_first(k, strip):
        fold_put(k, 0, dot(onehot(96, 128, fold_slots), strip, (0, 0)))

    def fold_next(k, step):
        value = fold_take(k, step - 1)

        def facing(p):
            into = p % 16 // 2
            target = into // 2 * 16 + p // 16 * 2 + into % 2
            shift = jnp.where(u == 6, 1, 0) - jnp.where(u == 7, 1, 0)
            source = (part[...] + ia - target + shift + LANES) % LANES
            return source // 2 % 8 * 16 + (source // 16 * 2 + source % 2) * 2 + p % 2

        matrix = onehot(128, 128, facing if step == 2 else fold_swap)
        fold_send(k, step, dot(matrix, value, (0, 0)))

    def fold_last(k):
        return dot(onehot(128, PAD * WIDE, fold_cells), fold_take(k, 3), (0, 0))

    @pl.when(top)
    def _():
        fold_first(0, xs[4:7].reshape(96, CH))

    pl.semaphore_wait(barrier, 35 + jnp.where(top, 14, 0))

    def halo(src, w, e, v, send, recv):
        return (
            remote(src.at[5:8], v.at[0], send.at[0], recv.at[0], north),
            remote(src.at[0:3], v.at[1], send.at[1], recv.at[1], south),
            remote(src.at[:, 16:32], w, send.at[2], recv.at[2], east),
            remote(src.at[:, 0:16], e, send.at[3], recv.at[3], west),
        )

    def start_south(copies):
        @pl.when(jnp.logical_not(bottom))
        def _():
            copies[1].start()

    def start_rest(copies):
        @pl.when(jnp.logical_not(top))
        def _():
            copies[0].start()

        copies[2].start()
        copies[3].start()

    def finish_south(copies):
        @pl.when(jnp.logical_not(bottom))
        def _():
            copies[1].wait_send()
            copies[0].wait_recv()

    def finish_north(copies):
        @pl.when(jnp.logical_not(top))
        def _():
            copies[0].wait_send()
            copies[1].wait_recv()

    def corners(v, w, e, send, recv):
        copies = []
        for k in range(2):
            copies.append(remote(v.at[k, :, 16:32], w.at[k], send.at[2 * k], recv.at[2 * k], east))
            copies.append(remote(v.at[k, :, 0:16], e.at[k], send.at[2 * k + 1], recv.at[2 * k + 1], west))
        return copies

    def rows_arrived(dst, copies, v, w, e, send, recv):
        passed = corners(v, w, e, send, recv)
        finish_south(copies)
        passed[0].start()
        passed[1].start()
        widen_rows(dst, v, 0)
        finish_north(copies)

        @pl.when(jnp.logical_not(top))
        def _():
            passed[2].start()
            passed[3].start()
            widen_rows(dst, v, 1)

        return passed

    def finish_corners_south(dst, copies, w, e):
        copies[0].wait()
        copies[1].wait()
        widen_corners(dst, w, e, 0)

    def finish_corners_north(dst, copies, w, e):
        @pl.when(jnp.logical_not(top))
        def _():
            copies[2].wait()
            copies[3].wait()
            widen_corners(dst, w, e, 1)

    first = halo(state, hw, he, hv, hs, hr)

    @pl.when(top)
    def _():
        fold_start(0, 0)

    start_south(first)
    start_rest(first)

    @pl.when(top)
    def _():
        fold_next(0, 1)

    @pl.when(bottom)
    def _():
        hv[0] = jnp.zeros((PAD, COLS, CH), BF16)

    own, south_rows, north_rows = tuple(range(PAD, PAD + ROWS)), (0, 1, 2), (11, 12, 13)
    every = tuple(range(ROWS))

    def nothing(ct, j):
        return jnp.zeros((COLS, 128), F32)

    def read_acc(ct, j):
        return acc[ct, j]

    def write_acc(ct, lanes, j, value):
        acc[ct, j] = value

    for copy in first[2:]:
        copy.wait()
    widen_sides(wide, hw, he)
    conv_part(wide, taps, False, own, every, nothing, write_acc)

    @pl.when(top)
    def _():
        fold_next(0, 2)

    second = rows_arrived(wide, first, hv, cw, ce, qs, qr)

    @pl.when(top)
    def _():
        fold_next(0, 3)

    def half_pass(k):
        base = k * 128
        block = slice(base, base + 128)
        beyond = (south_rows, north_rows)[k]
        conv_part(wide, taps, False, beyond, every[4 * k : 4 * k + 4], read_acc, write_acc)

        def norm_rows(i, _):
            cells = pl.ds(pl.multiple_of(base + i * 32, 32), 32)
            value = jnp.concatenate([acc[ct, 4 * k + i] for ct in range(3)], axis=1)
            value = value - jnp.mean(value, axis=1, keepdims=True)
            r = lax.rsqrt(jnp.mean(value * value, axis=1, keepdims=True) + 1e-06)
            value = value * r
            rstd[cells, :] = r
            unit[cells, :] = value
            normed[cells, :] = (value * gain[...][None] + shift[...][None]).astype(BF16)
            return 0

        lax.fori_loop(0, 4, norm_rows, 0, unroll=True)
        pre[...] = dot(normed[block, :], wup[...])

        def gelu_rows(i, totals):
            here = pl.ds(pl.multiple_of(i * 32, 32), 32)
            cells = pl.ds(pl.multiple_of(base + i * 32, 32), 32)
            done = []
            for q in range(3):
                lanes = slice(q * 256, q * 256 + 256)
                v = pre[here, lanes] + bup[:, lanes]
                square = v * v
                tanh = jnp.tanh(v * (COEFF + COEFF * CUBIC * square))
                half = 0.5 + 0.5 * tanh
                value = v * half
                slope = half + value * (1.0 - tanh) * (COEFF + 3.0 * CUBIC * COEFF * square)
                hidden[cells, lanes] = value.astype(BF16)
                grad = dhid[cells, lanes] * slope
                dpre[cells, lanes] = grad.astype(BF16)
                done.append(totals[q] + sub8(grad))
            return tuple(done)

        bias = lax.fori_loop(0, 4, gelu_rows, tuple(jnp.zeros((8, 256), F32) for _ in range(3)), unroll=True)
        dnorm[...] = dot(dpre[block, :], wup[...], (1, 1))

        def back_rows(i, totals):
            here = pl.ds(pl.multiple_of(i * 32, 32), 32)
            cells = pl.ds(pl.multiple_of(base + i * 32, 32), 32)
            unit_rows = unit[cells, :]
            grad = dnorm[here, :]
            product = grad * unit_rows
            scaled = grad * gain[...][None]
            mean_a = jnp.mean(scaled, axis=1, keepdims=True)
            mean_b = jnp.mean(product * gain[...][None], axis=1, keepdims=True)
            value = rstd[cells, :] * (scaled - mean_a - unit_rows * mean_b)
            value = value.astype(BF16)
            dcb[4 * k + i] = value
            value = value.astype(F32)
            for ct in range(3):
                dcv[ct, 4 * k + i] = value[:, ct * 128 : ct * 128 + 128]
            return totals[0] + sub8(product), totals[1] + sub8(grad)

        zero = jnp.zeros((8, CH), F32)
        return bias, lax.fori_loop(0, 4, back_rows, (zero, zero), unroll=True)

    @pl.when(bottom)
    def _():
        dv[0] = jnp.zeros((PAD, COLS, CH), BF16)

    finish_corners_south(wide, second, cw, ce)
    bias_a, norm_a = half_pass(0)
    third = halo(dcb, dw, de, dv, ds, dr)
    start_south(third)

    finish_corners_north(wide, second, cw, ce)

    @pl.when(top)
    def _():
        ghost = fold_last(0)
        for ct in range(3):
            for q in range(PAD):
                wide[ct, ROWS + PAD + q] = ghost[q * WIDE : (q + 1) * WIDE, ct * 128 : ct * 128 + 128]

    bias_b, norm_b = half_pass(1)

    start_rest(third)

    @pl.when(top)
    def _():
        fold_first(1, dcb[5:8].reshape(96, CH))
        fold_start(1, 0)

    def tap_tile(ct, _):
        lanes = pl.ds(pl.multiple_of(ct * 128, 128), 128)
        for b in range(KW):
            total = [jnp.zeros((8, 128), F32) for _ in range(KW)]
            for r in range(ROWS + 2 * PAD):
                value = wide[ct, r, 5 + b : 5 + b + COLS, :]
                for a in range(KW):
                    j = r - a
                    if 0 <= j < ROWS:
                        total[a] = total[a] + sub8(value * dcv[ct, j])
            for a in range(KW):
                s[a * KW + b : a * KW + b + 1, lanes] = jnp.sum(total[a], axis=0, keepdims=True)
        return 0

    s[...] = jnp.zeros((64, 512), F32)
    lax.fori_loop(0, 3, tap_tile, 0)

    branch = dot(hidden[...], wdown[...], (1, 1)) + bdown[...][None]
    g_scale = jnp.sum(masked[...] * branch, axis=0, keepdims=True)
    g_bup = jnp.concatenate(
        [jnp.sum(va + vb, axis=0, keepdims=True) for va, vb in zip(bias_a, bias_b)], axis=1
    )
    back = jnp.sum(dot(split3(g_bup), perm[...], (1, 1)), axis=0, keepdims=True)
    s[49:50, 0:CH] = jnp.sum(norm_a[0] + norm_b[0], axis=0, keepdims=True)
    s[50:51, 0:CH] = jnp.sum(norm_a[1] + norm_b[1], axis=0, keepdims=True)
    s[51:52, 0:CH] = jnp.sum(g_bdown, axis=0, keepdims=True)
    s[52:53, 0:CH] = g_scale
    s[53:54, 0:CH] = back[:, 0:CH]
    s[54:55, 0:CH] = back[:, CH:HID]
    half_s = pl.multiple_of((1 - c) * 32, 32)
    cross_s = remote(s.at[pl.ds(half_s, 32)], sc, sa_s.at[0], sa_r.at[0], other)
    cross_s.start()

    for half in range(2):
        units = slice(half * 384, half * 384 + 384)
        g[0, half] = dot(dpre[:, units], normed[...], (0, 0)).astype(BF16)
        g[1, half] = dot(dbr[...], hidden[:, units], (0, 0)).astype(BF16)
    cross = remote(g.at[:, 1 - c], gc, cs_s.at[0], cs_r.at[0], other)
    cross.start()

    cross_s.wait()
    mine_s = pl.multiple_of(c * 32, 32)
    s1[...] = (s[pl.ds(mine_s, 32), :] + sc[...]).reshape(4, 8, 512)
    small = []
    for d in range(1, 16):
        chunk = pl.ds(pl.multiple_of(lax.rem(y + d % 4, 4) * 128, 128), 128)
        piece = s1.at[lax.rem(x + d // 4, 4), :, chunk]
        copy = remote(piece, sx.at[d - 1], sx_s.at[d - 1], sx_r.at[d - 1], peer_xy(d))
        copy.start()
        small.append(copy)

    cross.wait()
    for k in range(2):
        for q in range(4):
            rows = slice(q * 96, q * 96 + 96)
            h[k, q] = (g[k, c, rows, :].astype(F32) + gc[k, rows, :].astype(F32)).astype(BF16)
    along = []
    for d in range(1, 4):
        up = remote(h.at[0, lax.rem(x + d, 4)], h1.at[0, d - 1], f_s.at[0, d - 1], f_r.at[0, d - 1], peer_x(d))
        down = remote(h.at[1, lax.rem(y + d, 4)], h1.at[1, d - 1], f_s.at[1, d - 1], f_r.at[1, d - 1], peer_y(d))
        up.start()
        down.start()
        along += [up, down]

    @pl.when(top)
    def _():
        fold_next(1, 1)

    def put_back(ct, lanes, j, value):
        value = cs[j, :, lanes].astype(F32) + value
        gs_out[j, :, lanes] = value.astype(BF16)
        if 4 <= j < 7:
            edge_rows[j - 4, :, lanes] = value

    def write_bacc(ct, lanes, j, value):
        if 3 <= j < 5:
            put_back(ct, lanes, j, value)
        else:
            bacc[ct, j] = value

    def read_bacc(ct, j):
        return bacc[ct, j]

    widen_own(dwide, dcb)

    for copy in small:
        copy.wait()
    mine_y = pl.ds(pl.multiple_of(y * 128, 128), 128)
    total = s1[x, :, mine_y]
    for q in range(15):
        total = total + sx[q]
    s3[...] = total
    small = []
    for d in range(1, 16):
        copy = remote(s3, sz.at[z], sz_s.at[d - 1], sz_r.at[d - 1], peer_z(d))
        copy.start()
        small.append(copy)
    sz[z] = s3[...]

    for copy in along:
        copy.wait()
    spread = onehot(CH, 512, lambda p: jnp.where(p % 128 < 96, p // 128 * 96 + p % 128, -1))
    for k in range(2):
        mine = h[k, (x, y)[k]].astype(F32)
        mine = mine + h1[k, 0].astype(F32) + h1[k, 1].astype(F32) + h1[k, 2].astype(F32)
        mine = dot(mine.astype(BF16), spread).astype(BF16)
        for q in range(4):
            h2[k, q] = mine[:, q * 128 : q * 128 + 128]
    along = []
    for d in range(1, 4):
        up = remote(h2.at[0, lax.rem(y + d, 4)], r2.at[0, d - 1], k_s.at[0, d - 1], k_r.at[0, d - 1], peer_y(d))
        down = remote(h2.at[1, lax.rem(x + d, 4)], r2.at[1, d - 1], k_s.at[1, d - 1], k_r.at[1, d - 1], peer_x(d))
        up.start()
        down.start()
        along += [up, down]

    for copy in third[2:]:
        copy.wait()
    widen_sides(dwide, dw, de)
    conv_part(dwide, taps, True, own, every, nothing, write_bacc)

    for copy in along:
        copy.wait()
    parts = []
    for k in range(2):
        mine = h2[k, (y, x)[k]].astype(F32)
        mine = mine + r2[k, 0].astype(F32) + r2[k, 1].astype(F32) + r2[k, 2].astype(F32)
        parts.append(mine.astype(BF16))
    pick_up = onehot(128, 256, lambda p: jnp.where(p % 128 < 48, p // 128 * 48 + p % 128, -1))
    pick_down = onehot(
        96, 256, lambda p: jnp.where((p % 128 >= 64) & (p % 128 < 112), p // 128 * 48 + p % 128 - 64, -1)
    )
    both = dot(parts[0], pick_up) + dot(parts[1], pick_down, (0, 0))[0:96]
    rows_to = onehot(96, 128, lambda p: jnp.where(p % 16 < 12, p // 16 * 12 + p % 16, -1))
    tiles = dot(rows_to, both.astype(BF16), (0, 0)).astype(BF16)
    for q in range(16):
        t[q] = tiles[q % 8 * 16 : q % 8 * 16 + 16, q // 8 * 128 : q // 8 * 128 + 128]
    along = []
    for d in range(1, 16):
        copy = remote(t.at[lax.rem(z + d, 16)], tz.at[d - 1], z_s.at[d - 1], z_r.at[d - 1], peer_z(d))
        copy.start()
        along.append(copy)

    @pl.when(top)
    def _():
        fold_next(1, 2)

    for copy in small:
        copy.wait()
    total = sz[0]
    for q in range(1, 16):
        total = total + sz[q]
    b2[x, :, mine_y] = total * FACTOR
    gather = []
    for d in range(1, 16):
        piece = b2.at[x, :, mine_y]
        copy = remote(piece, piece, gx_s.at[d - 1], gx_r.at[d - 1], peer_xy(d))
        copy.start()
        gather.append(copy)

    fourth = rows_arrived(dwide, third, dv, ew, ee, es, er)

    @pl.when(top)
    def _():
        dwide[:, ROWS + PAD :] = jnp.zeros((3, PAD, WIDE, 128), F32)

    @pl.when(top)
    def _():
        fold_next(1, 3)

    finish_corners_south(dwide, fourth, ew, ee)
    finish_corners_north(dwide, fourth, ew, ee)
    conv_part(dwide, taps, True, south_rows + north_rows, every, read_bacc, put_back)

    for copy in gather:
        copy.wait()
    b3[c] = b2[...]
    last = remote(b2, b3.at[c], gc_s.at[0], gc_r.at[0], other)
    last.start()

    for copy in along:
        copy.wait()
    total = t[z].astype(F32)
    for d in range(15):
        total = total + tz[d].astype(F32)
    tile_out[...] = total * FACTOR

    @pl.when(top)
    def _():
        ghost = fold_last(1)
        for ct in range(3):
            for q in range(PAD):
                edge[ct, q] = ghost[q * WIDE : (q + 1) * WIDE, ct * 128 : ct * 128 + 128]

        def read_edge(j, lanes):
            return edge_rows[j, :, lanes]

        def put_edge(j, lanes, value):
            gs_out[4 + j, :, lanes] = value.astype(BF16)

        fold_into(edge, taps, read_edge, put_edge)

    last.wait()
    small_out[...] = b3[...].reshape(64, 512)


def finish(gs_in, tile_in, small_in, gs_out, up_out, down_out, gk_out, gc_out, gb_out):
    gs_out[...] = gs_in[...]
    up_out[...] = tile_in[0:12, 0:48]
    down_out[...] = tile_in[0:12, 64:112]
    gk_out[...] = small_in[0:49, 0:CH]
    gc_out[...] = small_in[49:53, 0:CH]
    gb_out[0:CH] = small_in[53, 0:CH]
    gb_out[CH:HID] = small_in[54, 0:CH]


def fused(*args):
    sds = jax.ShapeDtypeStruct
    vm = pltpu.VMEM
    dma = pltpu.SemaphoreType.DMA
    hbm_spec = pl.BlockSpec(memory_space=pltpu.HBM)
    vm_spec = pl.BlockSpec(memory_space=pltpu.VMEM)
    edge16 = (ROWS, 16, CH)
    corner = (2, PAD, 16, CH)
    scratch = [
        vm((ROWS, COLS, CH), BF16), vm((ROWS, COLS, CH), BF16), vm((ROWS, COLS), jnp.int32), vm((1, 1), jnp.int32),
        vm((49, CH), F32), vm((CH,), F32), vm((CH,), F32), vm((CH, HID), BF16), vm((HID,), F32),
        vm((CH, HID), BF16), vm((CH,), F32), vm((CH,), F32),
        vm(edge16, BF16), vm(edge16, BF16), vm((2, PAD, COLS, CH), BF16), vm(corner, BF16), vm(corner, BF16),
        vm(edge16, BF16), vm(edge16, BF16), vm((2, PAD, COLS, CH), BF16), vm(corner, BF16), vm(corner, BF16),
        vm((3, 14, WIDE, 128), F32), vm((3, 14, WIDE, 128), F32), vm((3, PAD, WIDE, 128), F32),
        vm((3, ROWS, COLS, 128), F32), vm((3, ROWS, COLS, 128), F32), vm((PAD, COLS, CH), F32),
        vm((CH, HID), BF16), vm((CH, HID), BF16), vm((1, HID), F32),
        vm((CELLS, CH), F32), vm((CELLS, 1), F32), vm((CELLS, CH), BF16),
        vm((CELLS, CH), F32), vm((CELLS, CH), BF16), vm((CELLS, HID), F32), vm((CELLS // 2, HID), F32),
        vm((CELLS, HID), BF16), vm((CELLS, HID), BF16), vm((CELLS // 2, CH), F32),
        vm((3, ROWS, COLS, 128), F32), vm((ROWS, COLS, CH), BF16),
        vm((2, 2, 384, 384), BF16), vm((2, 384, 384), BF16), vm((2, 4, 96, 384), BF16),
        vm((2, 3, 96, 384), BF16), vm((2, 4, 96, 128), BF16), vm((2, 3, 96, 128), BF16),
        vm((16, 16, 128), BF16), vm((15, 16, 128), BF16), vm((HID, HID), BF16),
        vm((64, 512), F32), vm((32, 512), F32), vm((4, 8, 512), F32), vm((15, 8, 128), F32),
        vm((8, 128), F32), vm((16, 8, 128), F32), vm((4, 8, 512), F32),
        vm((2, 4, 8, 512), F32), vm((2, 4, 2, 8, 16, CH), BF16),
        dma((12,)), dma((4,)), dma((4,)), dma((4,)), dma((4,)), dma((4,)), dma((4,)), dma((4,)), dma((4,)),
        dma((1,)), dma((1,)), dma((2, 3)), dma((2, 3)), dma((2, 3)), dma((2, 3)), dma((15,)), dma((15,)),
        dma((1,)), dma((1,)), dma((15,)), dma((15,)), dma((15,)), dma((15,)),
        dma((15,)), dma((15,)), dma((1,)), dma((1,)), dma((2, 4, 7)), dma((2, 4, 7)),
    ]
    return pl.pallas_call(
        body,
        out_shape=[sds((ROWS, COLS, CH), BF16), sds((16, 128), F32), sds((64, 512), F32)],
        in_specs=[hbm_spec] * 12,
        out_specs=[vm_spec] * 3,
        scratch_shapes=scratch,
        compiler_params=pltpu.CompilerParams(
            collective_id=0, has_side_effects=True, vmem_limit_bytes=63 * 2**20
        ),
        name="block",
    )(*args)


def local(
    state, cotangent, ocean, fold_partner, kernel, ln_gain, ln_shift, w_up, b_up, w_down, b_down, layer_scale
):
    results = fused(
        state, cotangent, ocean, fold_partner[None], kernel, ln_gain, ln_shift, w_up, b_up,
        w_down, b_down, layer_scale,
    )
    sds = jax.ShapeDtypeStruct
    grad_state, up, down, g_kernel, g_chan, g_bup = (
        pl.pallas_call(
            finish,
            out_shape=[
                sds((ROWS, COLS, CH), BF16), sds((12, 48), F32), sds((12, 48), F32),
                sds((49, CH), F32), sds((4, CH), F32), sds((HID,), F32),
            ],
            name="outputs",
        )(*results)
    )
    return grad_state, up.T, down.T, g_kernel, g_chan, g_bup


def solution(mesh):
    placed = (P("ja", "ia", None), P("ja", "ia", None), P("ja", "ia"), P("ia")) + (P(),) * 8
    return jax.shard_map(
        local,
        mesh=mesh,
        in_specs=placed,
        out_specs=(P("ja", "ia", None), P("ja", "ia"), P("ja", "ia"), P(), P(), P()),
        check_vma=False,
    )
```
